32 devices in a mesh: gz: 4 (over y, x), xy: 8 (over z, core).
Axes of the slice: x: 2, y: 2, z: 4, core: 2. Of those that a mesh axis runs over, the one named last changes fastest.
Arguments:
- populations: float32 [19, 128, 32, 128], P(None, 'gz', 'xy'), as said below
- field_gain: float32 [128], P('gz'), may hold values from 0.05 to 0.4
- front_depth: int32 [8, 32], P('xy'), may hold values from 0 to 31, as said below
- phase: float32 [32, 256, 1024], P(None, 'xy', 'gz'), may hold values from 0 to 1
- solute: float32 [32, 256, 1024], P(None, 'xy', 'gz'), may hold values from 0.5 to 1.5
Outputs:
- velocity: float32 [3, 128, 32, 128], P(None, 'gz', 'xy')
- phase_next: float32 [32, 256, 1024], P(None, 'xy', 'gz')
- solute_next: float32 [32, 256, 1024], P(None, 'xy', 'gz')
The draws below stay inside these ranges and needn't reach their ends.
Inputs may be any that keep to these rules, and one draw needn't show every extreme that they name: Every cell's populations are positive and within a fifth of a lattice equilibrium of density near 1 and speed below 0.2. `front_depth`: depth indices of the front tiles, from 0 to 31.
All inputs are finite; a program needn't handle non-finite values.
Results may differ from the reference program's by a relative error of at most 0.0003.
Values sent between devices are 32-bit elements; how exact they have to be, the bound alone decides.
A program may use at most 128 MiB of HBM per device.

```python
import math
import jax
import jax.numpy as jnp
import numpy as np
from jax import lax

NYC = 128
BAND = 32
NZC = 128
NXC = 32
NXF = 256
NYF = 1024


sample_dirs = np.array([[0, 0, 0], [1, 0, 0], [-1, 0, 0], [0, 1, 0], [0, -1, 0], [0, 0, 1], [0, 0, -1], [1, 1, 0], [-1, -1, 0], [1, -1, 0], [-1, 1, 0], [1, 0, 1], [-1, 0, -1], [1, 0, -1], [-1, 0, 1], [0, 1, 1], [0, -1, -1], [0, 1, -1], [0, -1, 1]], dtype=np.float32)


sample_weights = np.array([1.0 / 3.0] + [1.0 / 18.0] * 6 + [1.0 / 36.0] * 12, dtype=np.float32)


def draw_populations(key, part):
    key_density, key_flow, key_noise = jax.random.split(key, 3)
    grid = (NZC, NXC, NYC)
    density = 1.0 + 0.15 * jax.random.uniform(key_density, grid, jnp.float32, -1.0, 1.0)
    flow = 0.1 * jax.random.uniform(key_flow, (3,) + grid, jnp.float32, -1.0, 1.0)
    directions = jnp.asarray(sample_dirs)
    weights = jnp.asarray(sample_weights)[:, None, None, None]
    along = directions[:, 0, None, None, None] * flow[0][None] + directions[:, 1, None, None, None] * flow[1][None] + directions[:, 2, None, None, None] * flow[2][None]
    speed = flow[0] * flow[0] + flow[1] * flow[1] + flow[2] * flow[2]
    equil = weights * density[None] * (1.0 + 3.0 * along + 4.5 * along * along - 1.5 * speed[None])
    noise = 1.0 + 0.2 * jax.random.uniform(key_noise, (19,) + grid, jnp.float32, -1.0, 1.0)
    return (equil * noise).astype(jnp.float32)


def draw_front_depth(key, part):
    tiles_z = NZC // 4
    key_center, key_offset = jax.random.split(key)
    center = jax.random.randint(key_center, (), tiles_z // 4, tiles_z - tiles_z // 4)
    offset = jax.random.randint(key_offset, (NXC // 4, NYC // 4), -2, 3)
    depth = jnp.clip(center + offset, 0, tiles_z - 1)
    depth = depth.at[0, 0].set(0)
    depth = depth.at[NXC // 4 - 1, NYC // 4 - 1].set(tiles_z - 1)
    return depth.astype(jnp.int32)


def block_scale(key, shape, pieces, low, largest):
    level = 1.0
    for position, shards_of in pieces:
        heights = jax.random.uniform(jax.random.fold_in(jax.random.fold_in(key, 6), position), (shards_of,), jnp.float32, low / len(pieces), largest / len(pieces))
        level = level * jnp.repeat(jnp.exp(heights), shape[position] // shards_of).reshape((-1,) + (1,) * (len(shape) - 1 - position))
    return level


def setup_inputs(seed: int = 0) -> dict:
    streams_of = jax.random.split(jax.random.key(seed), 6)
    return {
        "populations": draw_populations(jax.random.fold_in(streams_of[5], 71), 0),
        "field_gain": jnp.clip(jnp.exp(math.log(0.4) - 2.0794415 * jax.random.uniform(streams_of[1], (NZC,), jnp.float32) ** block_scale(streams_of[1], (NZC,), ((0, 4),), -0.2, 0.2)), 0.05, 0.4),
        "front_depth": draw_front_depth(jax.random.fold_in(streams_of[5], 71), 0),
        "phase": jnp.clip(1.0 * jax.random.uniform(streams_of[3], (BAND, NXF, NYF), jnp.float32) ** block_scale(streams_of[3], (BAND, NXF, NYF), ((1, 8), (2, 4)), -0.2, 0.2), 0.0, 1.0),
        "solute": jnp.clip(0.5 + 1.0 * jax.random.uniform(streams_of[4], (BAND, NXF, NYF), jnp.float32) ** block_scale(streams_of[4], (BAND, NXF, NYF), ((1, 8), (2, 4)), -0.2, 0.2), 0.5, 1.5),
    }


lattice_dirs = np.array([[0, 0, 0], [1, 0, 0], [-1, 0, 0], [0, 1, 0], [0, -1, 0], [0, 0, 1], [0, 0, -1], [1, 1, 0], [-1, -1, 0], [1, -1, 0], [-1, 1, 0], [1, 0, 1], [-1, 0, -1], [1, 0, -1], [-1, 0, 1], [0, 1, 1], [0, -1, -1], [0, 1, -1], [0, -1, 1]], dtype=np.int64)
lattice_weights = np.array([1.0 / 3.0] + [1.0 / 18.0] * 6 + [1.0 / 36.0] * 12)
relax_time = 0.8
field_phase = 0.7
time_step = 0.1
depth_weight = 1.5
growth_rate = 4.0
advect_scale = 4.0
solute_shift = 0.5
solute_ref = 1.0
partition = 0.15


def lorentz(gain, x_pos, y_pos, width_x, width_y):
    angle_x = (2.0 * math.pi / width_x) * (x_pos + 0.5)
    angle_y = (2.0 * math.pi / width_y) * (y_pos + 0.5)
    scale = gain[:, None, None]
    along_x = angle_x[None, :, None]
    along_y = angle_y[None, None, :]
    full_shape = (gain.shape[0], x_pos.shape[0], y_pos.shape[0])
    first = jnp.broadcast_to(scale * jnp.cos(along_x - field_phase), full_shape)
    second = jnp.broadcast_to(scale * jnp.sin(along_y + field_phase), full_shape)
    third = scale * jnp.cos(along_x + along_y)
    return jnp.stack([first, second, third])


def flow_velocity(populations, force):
    directions = jnp.asarray(lattice_dirs, jnp.float32)
    density = jnp.sum(populations, axis=0)
    moment = jnp.einsum("qc,qzxy->czxy", directions, populations, precision=lax.Precision.HIGHEST)
    return (moment + 0.5 * force) / density


def collide(populations, force):
    directions = jnp.asarray(lattice_dirs, jnp.float32)
    weights = jnp.asarray(lattice_weights, jnp.float32)[:, None, None, None]
    density = jnp.sum(populations, axis=0)
    flow = flow_velocity(populations, force)
    along = jnp.einsum("qc,czxy->qzxy", directions, flow, precision=lax.Precision.HIGHEST)
    push = jnp.einsum("qc,czxy->qzxy", directions, force, precision=lax.Precision.HIGHEST)
    speed = jnp.sum(flow * flow, axis=0)
    work = jnp.sum(flow * force, axis=0)
    equil = weights * density * (1.0 + 3.0 * along + 4.5 * along * along - 1.5 * speed)
    source = (1.0 - 0.5 / relax_time) * weights * (3.0 * (push - work) + 9.0 * along * push)
    return populations - (populations - equil) / relax_time + source


def interp_table():
    fine_index = jnp.arange(32, dtype=jnp.int32)
    numer = 2 * fine_index + 9
    lower = numer // 16
    frac = (numer % 16).astype(jnp.float32) / 16.0
    coarse = jnp.arange(6, dtype=jnp.int32)
    first = (coarse[None, :] == lower[:, None]).astype(jnp.float32)
    second = (coarse[None, :] == lower[:, None] + 1).astype(jnp.float32)
    return (1.0 - frac)[:, None] * first + frac[:, None] * second


def stencil(field):
    deep = jnp.concatenate([field[:1], field, field[-1:]], axis=0)
    center = deep[1:-1, 1:-1, 1:-1]
    upper = deep[2:, 1:-1, 1:-1]
    below = deep[:-2, 1:-1, 1:-1]
    right = deep[1:-1, 2:, 1:-1]
    left = deep[1:-1, :-2, 1:-1]
    ahead = deep[1:-1, 1:-1, 2:]
    behind = deep[1:-1, 1:-1, :-2]
    second_z = upper + below - 2.0 * center
    second_x = right + left - 2.0 * center
    second_y = ahead + behind - 2.0 * center
    return center, second_z, second_x, second_y, 0.5 * (upper - below), 0.5 * (right - left), 0.5 * (ahead - behind)


def advance(phase_pad, solute_pad, flow):
    phase_mid, phase_zz, phase_xx, phase_yy, phase_dz, phase_dx, phase_dy = stencil(phase_pad)
    sol_mid, sol_zz, sol_xx, sol_yy, sol_dz, sol_dx, sol_dy = stencil(solute_pad)
    drift_phase = flow[0] * phase_dz + flow[1] * phase_dx + flow[2] * phase_dy
    drift_sol = flow[0] * sol_dz + flow[1] * sol_dx + flow[2] * sol_dy
    drive = growth_rate * phase_mid * (1.0 - phase_mid) * (phase_mid - 0.5 + solute_shift * (sol_mid - solute_ref))
    phase_new = phase_mid + time_step * (depth_weight * phase_zz + phase_xx + phase_yy - advect_scale * drift_phase + drive)
    sol_new = sol_mid + time_step * (sol_zz + sol_xx + sol_yy - advect_scale * drift_sol) + (1.0 - partition) * sol_mid * (phase_new - phase_mid)
    return phase_new, sol_new


def wrap_cols(field):
    return jnp.concatenate([field[..., -1:], field, field[..., :1]], axis=-1)


def reference(populations, field_gain, front_depth, phase, solute):
    depth_c = populations.shape[1]
    rows_c = populations.shape[2]
    cols_c = populations.shape[3]
    force = lorentz(field_gain, jnp.arange(rows_c).astype(jnp.float32), jnp.arange(cols_c).astype(jnp.float32), rows_c, cols_c)
    post = collide(populations, force)
    moved = []
    for direction in range(19):
        step_z, step_x, step_y = (int(v) for v in lattice_dirs[direction])
        moved.append(jnp.roll(post[direction], (step_z, step_x, step_y), axis=(0, 1, 2)))
    velocity = flow_velocity(jnp.stack(moved), force)
    table = interp_table()
    tiles_x = rows_c // 4
    tiles_y = cols_c // 4
    fine_x = rows_c * 8
    fine_y = cols_c * 8
    offsets = jnp.arange(6, dtype=jnp.int32)

    def fine_flow(tile_x):
        tile_x = tile_x % tiles_x
        depth_row = front_depth[tile_x].astype(jnp.int32)
        z_index = (depth_row[:, None] * 4 - 1 + offsets[None, :]) % depth_c
        x_index = (tile_x * 4 - 1 + offsets) % rows_c
        y_index = (jnp.arange(tiles_y, dtype=jnp.int32)[:, None] * 4 - 1 + offsets[None, :]) % cols_c
        window = velocity[:, z_index[:, :, None, None], x_index[None, None, :, None], y_index[:, None, None, :]]
        result = jnp.einsum("kz,Xx,Yy,cbzxy->ckXbY", table, table, table, window, precision=lax.Precision.HIGHEST)
        return result.reshape(3, 32, 32, fine_y)

    rim_offsets = jnp.arange(36, dtype=jnp.int32)

    def slab(tile_x):
        flow_rows = jnp.concatenate([fine_flow(tile_x - 1), fine_flow(tile_x), fine_flow(tile_x + 1)], axis=2)[:, :, 31:65]
        rows = (tile_x * 32 - 2 + rim_offsets) % fine_x
        phase_rows = jnp.take(phase, rows, axis=1)
        sol_rows = jnp.take(solute, rows, axis=1)
        phase_one, sol_one = advance(wrap_cols(phase_rows), wrap_cols(sol_rows), flow_rows)
        return advance(wrap_cols(phase_one), wrap_cols(sol_one), flow_rows[:, :, 1:-1])

    phase_slabs, sol_slabs = lax.map(slab, jnp.arange(tiles_x, dtype=jnp.int32))
    phase_next = jnp.moveaxis(phase_slabs, 0, 1).reshape(32, fine_x, fine_y)
    solute_next = jnp.moveaxis(sol_slabs, 0, 1).reshape(32, fine_x, fine_y)
    return velocity, phase_next, solute_next
```

```python
import functools
import math

import jax
import jax.numpy as jnp
import numpy as np
from jax import lax
from jax.experimental import pallas as pl
from jax.experimental.pallas import tpu as pltpu
from jax.sharding import PartitionSpec as P

MESH = pl.DeviceIdType.MESH
F32 = jnp.float32

PAIRS = (
    (1, 2, (1, 0, 0), 1.0 / 18.0),
    (3, 4, (0, 1, 0), 1.0 / 18.0),
    (5, 6, (0, 0, 1), 1.0 / 18.0),
    (7, 8, (1, 1, 0), 1.0 / 36.0),
    (9, 10, (1, -1, 0), 1.0 / 36.0),
    (11, 12, (1, 0, 1), 1.0 / 36.0),
    (13, 14, (1, 0, -1), 1.0 / 36.0),
    (15, 16, (0, 1, 1), 1.0 / 36.0),
    (17, 18, (0, 1, -1), 1.0 / 36.0),
)


def weights_of(fine):
    numer = 2 * fine + 9
    return numer // 16, (numer % 16) / 16.0


def col_table():
    table = np.zeros((128, 512), np.float32)
    for par in range(2):
        for fine in range(256):
            tile, inner = fine // 32, fine % 32
            low, frac = weights_of(inner)
            for off, weight in ((low, 1.0 - frac), (low + 1, frac)):
                if off == 0:
                    rim, j = 1, 0
                elif off == 5:
                    rim, j = 1, 3
                else:
                    rim, j = 0, off - 1
                table[par * 64 + rim * 32 + tile * 4 + j, par * 256 + fine] += weight
    return table


def row_table():
    table = np.zeros((32, 8), np.float32)
    for fine in range(32):
        low, frac = weights_of(fine)
        for off, weight in ((low, 1.0 - frac), (low + 1, frac)):
            place = 4 if off == 0 else off if off == 5 else off - 1
            table[fine, place] += 0.2 * weight
    return table


def force_table(lanes, width_y):
    width_x = 4 * lanes
    x = (np.arange(width_x) + 0.5) * (2.0 * math.pi / width_x)
    y = (np.arange(width_y) + 0.5) * (2.0 * math.pi / width_y)
    ax = np.tile(x.reshape(lanes, 4), (1, 2))[:, :, None]
    ay = y[None, None, :]
    full = (lanes, 8, width_y)
    return np.stack(
        [
            np.broadcast_to(np.cos(ax - 0.7), full),
            np.broadcast_to(np.sin(ay + 0.7), full),
            np.cos(ax + ay),
        ],
        axis=1,
    ).astype(np.float32)


def kernel(
    slabs, lanes,
    pop, gain, depth, phase, solute, ftab, ctab, rtab,
    vel, p_out, s_out,
    sums, xs, xr, zr, dr, vs, vr, v8, v8r, pk, wr, fine, ex, hx, ey, hy, p1, s1,
    send, recv,
):
    gz, xy = lax.axis_index("gz"), lax.axis_index("xy")

    def at(dz, dx):
        return (lax.rem(gz + dz + slabs, slabs), lax.rem(xy + dx + lanes, lanes))

    peers = [(1, 0), (-1, 0), (0, 1), (0, -1), (1, 1), (1, -1), (-1, 1), (-1, -1)]
    peers += [(d, 0) for d in range(2, slabs - 1)]
    barrier = pltpu.get_barrier_semaphore()
    for peer in peers:
        pl.semaphore_signal(barrier, inc=1, device_id=at(*peer), device_id_type=MESH)

    count = [0]

    def remote(src, dst, where):
        i = count[0]
        count[0] += 1
        copy = pltpu.make_async_remote_copy(
            src_ref=src, dst_ref=dst, send_sem=send.at[i], recv_sem=recv.at[i],
            device_id=at(*where), device_id_type=MESH,
        )
        copy.start()
        return copy

    rows32 = lax.broadcasted_iota(jnp.int32, (128, 32), 0) // 4
    cols32 = lax.broadcasted_iota(jnp.int32, (128, 32), 1)
    gain_col = jnp.sum(jnp.where(rows32 == cols32, gain[...], 0.0), axis=1, keepdims=True)
    shape = ftab[xy]
    force = [
        jnp.broadcast_to(shape[c][None], (16, 8, 128)).reshape(128, 128) * gain_col
        for c in range(3)
    ]
    for c in range(3):
        vel[c] = force[c]

    def collide(i, carry):
        at_rows = pl.ds(pl.multiple_of(i * 8, 8), 8)
        f = [pop[q, at_rows, :] for q in range(19)]
        fc = [vel[c, at_rows, :] for c in range(3)]
        rho = f[0]
        mom = [0.5 * fc[0], 0.5 * fc[1], 0.5 * fc[2]]
        for a, b, e, _ in PAIRS:
            rho = rho + (f[a] + f[b])
            odd = f[a] - f[b]
            for c in range(3):
                if e[c] > 0:
                    mom[c] = mom[c] + odd
                elif e[c] < 0:
                    mom[c] = mom[c] - odd
        inv = 1.0 / rho
        u = [m * inv for m in mom]
        speed = u[0] * u[0] + u[1] * u[1] + u[2] * u[2]
        work = u[0] * fc[0] + u[1] * fc[1] + u[2] * fc[2]
        base = 1.25 * rho * (1.0 - 1.5 * speed) - 1.125 * work
        rho_a = 5.625 * rho
        rho_b = 3.75 * rho
        post = [None] * 19
        post[0] = -0.25 * f[0] + (1.0 / 3.0) * base

        def along(v, e):
            total = None
            for c in range(3):
                if e[c]:
                    term = v[c] if e[c] > 0 else -v[c]
                    total = term if total is None else total + term
            return total

        for a, b, e, w in PAIRS:
            cu, cf = along(u, e), along(fc, e)
            even = w * (base + cu * (rho_a * cu + 3.375 * cf))
            odd = w * (rho_b * cu + 1.125 * cf)
            post[a] = -0.25 * f[a] + (even + odd)
            post[b] = -0.25 * f[b] + (even - odd)

        def up(q):
            return pltpu.roll(post[q], 1, 1)

        def down(q):
            return pltpu.roll(post[q], 127, 1)

        def put(n, middle, plus, minus):
            a, b = up(plus), down(minus)
            sums[n, at_rows, :] = post[middle] + (a + b)
            sums[n + 1, at_rows, :] = a - b

        put(0, 1, 11, 13)
        sums[2, at_rows, :] = post[7]
        sums[3, at_rows, :] = post[9]
        put(4, 2, 14, 12)
        sums[6, at_rows, :] = post[10]
        sums[7, at_rows, :] = post[8]
        put(8, 3, 15, 17)
        put(10, 4, 18, 16)
        put(12, 0, 5, 6)
        return carry

    lax.fori_loop(0, 16, collide, 0)

    row = lax.broadcasted_iota(jnp.int32, (128, 128), 0)
    x_of = lax.rem(row, 4)
    plus_ids, minus_ids = (8, 9, 2, 6), (10, 11, 3, 7)

    def roll0(v, s):
        s = s % v.shape[0]
        return v if s == 0 else pltpu.roll(v, s, 0)

    def merge(values):
        out = values[-1]
        for m in range(len(values) - 1):
            out = jnp.where(x_of == m, values[m], out)
        return out

    xs[0] = merge([roll0(sums[i], m - 3) for m, i in enumerate(plus_ids)])
    xs[1] = merge([roll0(sums[i], m) for m, i in enumerate(minus_ids)])

    pl.semaphore_wait(barrier, len(peers))
    flow_copies = [
        remote(xs.at[0], xr.at[0], (0, 1)),
        remote(xs.at[1], xr.at[1], (0, -1)),
        remote(sums.at[pl.ds(0, 4), pl.ds(120, 8)], zr.at[0], (1, 0)),
        remote(sums.at[pl.ds(4, 4), pl.ds(0, 8)], zr.at[1], (-1, 0)),
        remote(sums.at[2, pl.ds(120, 8)], dr.at[0], (1, 1)),
        remote(sums.at[3, pl.ds(120, 8)], dr.at[1], (1, -1)),
        remote(sums.at[6, pl.ds(0, 8)], dr.at[2], (-1, 1)),
        remote(sums.at[7, pl.ds(0, 8)], dr.at[3], (-1, -1)),
    ]

    lane = lax.broadcasted_iota(jnp.int32, (32, 128), 1)

    def edges(k, carry):
        first, last = carry
        for n, ref in enumerate((phase, solute)):
            ex[0, 0, n, pl.ds(k, 1), :] = ref[k, 31:32, :]
            ex[0, 1, n, pl.ds(k, 1), :] = ref[k, 0:1, :]
            here = lane == k + 32 * n
            last = jnp.where(here, ref[k, :, 255:256], last)
            first = jnp.where(here, ref[k, :, 0:1], first)
        return first, last

    nothing = jnp.zeros((32, 128), F32)
    first, last = lax.fori_loop(0, 32, edges, (nothing, nothing))
    ey[0, 0] = last
    ey[0, 1] = first

    def send_edges(turn):
        return [
            remote(ex.at[turn, 0], hx.at[turn, 0], (0, 1)),
            remote(ex.at[turn, 1], hx.at[turn, 1], (0, -1)),
            remote(ey.at[turn, 0], hy.at[turn, 0], (1, 0)),
            remote(ey.at[turn, 1], hy.at[turn, 1], (-1, 0)),
        ]

    band_copies = send_edges(0)
    for copy in flow_copies:
        copy.wait()

    sub = lax.broadcasted_iota(jnp.int32, (8, 128), 0)

    def shift_x(i, sign):
        if sign > 0:
            m = plus_ids.index(i)
            return jnp.where(x_of == 0, roll0(xr[0], -m), roll0(sums[i], 1))
        m = minus_ids.index(i)
        return jnp.where(x_of == 3, roll0(xr[1], 3 - m), roll0(sums[i], -1))

    def shift_z(value, sign, block):
        moved = roll0(value, 4 * sign)
        if sign > 0:
            return jnp.concatenate([jnp.where(sub < 4, block, moved[:8]), moved[8:]], axis=0)
        return jnp.concatenate([moved[:120], jnp.where(sub >= 4, block, moved[120:])], axis=0)

    rho = sums[12]
    my = sums[13]
    a = shift_x(8, 1)
    b = shift_x(10, -1)
    rho = rho + (a + b)
    mx = a - b
    my = my + (shift_x(9, 1) + shift_x(11, -1))
    a = shift_z(sums[0], 1, roll0(zr[0, 0], 4))
    b = shift_z(sums[4], -1, roll0(zr[1, 0], 4))
    rho = rho + (a + b)
    mz = a - b
    my = my + shift_z(sums[1], 1, roll0(zr[0, 1], 4))
    my = my + shift_z(sums[5], -1, roll0(zr[1, 1], 4))
    a = shift_z(shift_x(2, 1), 1, jnp.where(sub == 0, roll0(dr[0], 1), roll0(zr[0, 2], 5)))
    b = shift_z(shift_x(7, -1), -1, jnp.where(sub == 7, roll0(dr[3], 7), roll0(zr[1, 3], 3)))
    rho = rho + (a + b)
    mz = mz + (a - b)
    mx = mx + (a - b)
    a = shift_z(shift_x(3, -1), 1, jnp.where(sub == 3, roll0(dr[1], 7), roll0(zr[0, 3], 3)))
    b = shift_z(shift_x(6, 1), -1, jnp.where(sub == 4, roll0(dr[2], 1), roll0(zr[1, 2], 5)))
    rho = rho + (a + b)
    mz = mz + (a - b)
    mx = mx - (a - b)
    inv = 1.0 / rho
    v = [(m + 0.5 * vel[c]) * inv for c, m in enumerate((mz, mx, my))]
    for c in range(3):
        vel[c] = v[c]
    vs[0] = merge([roll0(v[c], c - 3) for c in range(3)])
    vs[1] = merge([roll0(v[c], c) for c in range(3)])
    rim_copies = [
        remote(vs.at[0], vr.at[0], (0, 1)),
        remote(vs.at[1], vr.at[1], (0, -1)),
    ]
    for copy in rim_copies:
        copy.wait()

    sub128 = lax.rem(row, 8)
    lane128 = lax.broadcasted_iota(jnp.int32, (128, 128), 1)
    lane_in = lax.rem(lane128, 4)
    for c in range(3):
        own = vel[c]
        for par in range(2):
            block = jnp.where(
                sub128 == 4,
                roll0(vr[0], 4 - c - 4 * par),
                jnp.where(sub128 == 5, roll0(vr[1], 5 - c - 4 * par), roll0(own, -4 * par)),
            )
            v8[c, par] = block.reshape(16, 8, 128)
            side = jnp.where(lane_in == 0, pltpu.roll(block, 1, 1), pltpu.roll(block, 127, 1))
            v8r[c, par] = side.reshape(16, 8, 128)

    lane8 = lax.broadcasted_iota(jnp.int32, (8, 128), 1)
    tile_of = lane8 // 4
    group_of = lane8 // 32
    total_z = 32 * slabs
    none8 = jnp.zeros((8, 128), F32)
    for c in range(3):

        def gather(tile, carry):
            carry = list(carry)
            start = depth[0, tile] * 4 - 1 + total_z
            for dz in range(6):
                z = lax.rem(start + dz, total_z)
                z_here = lax.rem(z, 32)
                mark = jnp.where(z // 32 == gz, tile, -1)
                here = tile_of == mark
                par, half = lax.rem(z_here, 2), z_here // 2
                carry[2 * dz] = jnp.where(here, v8[c, par, half], carry[2 * dz])
                carry[2 * dz + 1] = jnp.where(here, v8r[c, par, half], carry[2 * dz + 1])
            return tuple(carry)

        items = lax.fori_loop(0, 8 * slabs, gather, (none8,) * 12)
        for target in range(slabs):
            for m in range(3):
                out = none8
                for g in range(4):
                    item = items[4 * m + g]
                    s = (32 * (g - target)) % 128
                    moved = item if s == 0 else pltpu.roll(item, s, 1)
                    out = jnp.where(group_of == g, moved, out)
                pk[target, 3 * c + m] = out

    window_copies = [
        remote(pk.at[lax.rem(gz + d, slabs)], wr.at[d - 1], (d, 0)) for d in range(1, slabs)
    ]
    windows = pk[gz]
    for d, copy in enumerate(window_copies):
        copy.wait()
        windows = windows + wr[d]
    wide = jnp.dot(
        windows.reshape(72, 128), ctab[...],
        precision=lax.Precision.HIGHEST, preferred_element_type=F32,
    )
    for c in range(3):
        for dz in range(6):
            at_row = (3 * c + dz // 2) * 8
            at_col = (dz % 2) * 256
            fine[c, dz] = jnp.dot(
                rtab[...], wide[at_row:at_row + 8, at_col:at_col + 256],
                precision=lax.Precision.HIGHEST, preferred_element_type=F32,
            )

    big_row = lax.broadcasted_iota(jnp.int32, (32, 256), 0)
    big_lane = lax.broadcasted_iota(jnp.int32, (32, 256), 1)

    def band(turn, src, dst):
        def plane(k, carry):
            before, after, first, last = carry
            low = (2 * k + 9) // 16
            frac = lax.rem(2 * k + 9, 16).astype(F32) * (1.0 / 16.0)
            flow = []
            for c in range(3):
                lower = fine[c, low]
                flow.append(lower + frac * (fine[c, low + 1] - lower))
            above, below = jnp.minimum(k + 1, 31), jnp.maximum(k - 1, 0)
            results = []
            for n, ref in enumerate(src):
                mid = ref[k]
                zu, zd = ref[above], ref[below]
                xu = jnp.where(
                    big_row == 31, hx[turn, 1, n, pl.ds(k, 1), :], pltpu.roll(mid, 31, 0)
                )
                xd = jnp.where(
                    big_row == 0, hx[turn, 0, n, pl.ds(k, 1), :], pltpu.roll(mid, 1, 0)
                )
                yu = jnp.where(
                    big_lane == 255, after[:, 32 * n:32 * n + 1], pltpu.roll(mid, 255, 1)
                )
                yd = jnp.where(
                    big_lane == 0, before[:, 32 * n:32 * n + 1], pltpu.roll(mid, 1, 1)
                )
                drift = flow[0] * (zu - zd) + flow[1] * (xu - xd) + flow[2] * (yu - yd)
                zz = zu + zd
                side = (xu + xd) + (yu + yd)
                results.append((mid, zz, side, drift))
            p, zz, side, drift = results[0]
            s = results[1][0]
            drive = p * (1.0 - p) * (0.4 * p + 0.2 * s - 0.4)
            change = 0.15 * zz + 0.1 * side - 0.7 * p - drift + drive
            p_new = p + change
            s, zz, side, drift = results[1]
            s_new = 0.4 * s + 0.1 * (zz + side) - drift + 0.85 * s * change
            dst[0][k] = p_new
            dst[1][k] = s_new
            if turn == 0:
                for n, new in enumerate((p_new, s_new)):
                    ex[1, 0, n, pl.ds(k, 1), :] = new[31:32, :]
                    ex[1, 1, n, pl.ds(k, 1), :] = new[0:1, :]
                    here = lane == k + 32 * n
                    last = jnp.where(here, new[:, 255:256], last)
                    first = jnp.where(here, new[:, 0:1], first)
            return pltpu.roll(before, 127, 1), pltpu.roll(after, 127, 1), first, last

        return lax.fori_loop(0, 32, plane, (hy[turn, 0], hy[turn, 1], nothing, nothing))

    for copy in band_copies:
        copy.wait()
    _, _, first, last = band(0, (phase, solute), (p1, s1))
    ey[1, 0] = last
    ey[1, 1] = first
    for copy in send_edges(1):
        copy.wait()
    band(1, (p1, s1), (p_out, s_out))


def body(slabs, lanes, populations, field_gain, front_depth, phase, solute):
    depth_here, rows_here, cols = populations.shape[1:]
    pops = populations.reshape(19, depth_here * rows_here, cols)
    vmem = pl.BlockSpec(memory_space=pltpu.VMEM)
    smem = pl.BlockSpec(memory_space=pltpu.SMEM)
    copies = 8 + 4 + 2 + (slabs - 1) + 4
    velocity, phase_next, solute_next = pl.pallas_call(
        functools.partial(kernel, slabs, lanes),
        out_shape=(
            jax.ShapeDtypeStruct((3, 128, 128), F32),
            jax.ShapeDtypeStruct(phase.shape, F32),
            jax.ShapeDtypeStruct(solute.shape, F32),
        ),
        in_specs=[vmem, vmem, smem, vmem, vmem, vmem, vmem, vmem],
        out_specs=(vmem, vmem, vmem),
        scratch_shapes=[
            pltpu.VMEM((14, 128, 128), F32),
            pltpu.VMEM((2, 128, 128), F32),
            pltpu.VMEM((2, 128, 128), F32),
            pltpu.VMEM((2, 4, 8, 128), F32),
            pltpu.VMEM((4, 8, 128), F32),
            pltpu.VMEM((2, 128, 128), F32),
            pltpu.VMEM((2, 128, 128), F32),
            pltpu.VMEM((3, 2, 16, 8, 128), F32),
            pltpu.VMEM((3, 2, 16, 8, 128), F32),
            pltpu.VMEM((slabs, 9, 8, 128), F32),
            pltpu.VMEM((slabs - 1, 9, 8, 128), F32),
            pltpu.VMEM((3, 6, 32, 256), F32),
            pltpu.VMEM((2, 2, 2, 32, 256), F32),
            pltpu.VMEM((2, 2, 2, 32, 256), F32),
            pltpu.VMEM((2, 2, 32, 128), F32),
            pltpu.VMEM((2, 2, 32, 128), F32),
            pltpu.VMEM((32, 32, 256), F32),
            pltpu.VMEM((32, 32, 256), F32),
            pltpu.SemaphoreType.DMA((copies,)),
            pltpu.SemaphoreType.DMA((copies,)),
        ],
        compiler_params=pltpu.CompilerParams(
            collective_id=0, has_side_effects=True, vmem_limit_bytes=40 * 2**20
        ),
    )(
        pops,
        field_gain.reshape(1, depth_here),
        front_depth,
        phase,
        solute,
        jnp.asarray(force_table(lanes, cols)),
        jnp.asarray(col_table()),
        jnp.asarray(row_table()),
    )
    return velocity.reshape(3, depth_here, rows_here, cols), phase_next, solute_next


def solution(mesh):
    return jax.shard_map(
        functools.partial(body, mesh.shape["gz"], mesh.shape["xy"]),
        mesh=mesh,
        in_specs=(
            P(None, "gz", "xy", None),
            P("gz"),
            P("xy", None),
            P(None, "xy", "gz"),
            P(None, "xy", "gz"),
        ),
        out_specs=(P(None, "gz", "xy", None), P(None, "xy", "gz"), P(None, "xy", "gz")),
        check_vma=False,
    )
```

```python
import functools
import math

import jax
import jax.numpy as jnp
import numpy as np
from jax import lax
from jax.experimental import pallas as pl
from jax.experimental.pallas import tpu as pltpu
from jax.sharding import PartitionSpec as P

MESH = pl.DeviceIdType.MESH
F32 = jnp.float32

PAIRS = (
    (1, 2, (1, 0, 0), 1.0 / 18.0),
    (3, 4, (0, 1, 0), 1.0 / 18.0),
    (5, 6, (0, 0, 1), 1.0 / 18.0),
    (7, 8, (1, 1, 0), 1.0 / 36.0),
    (9, 10, (1, -1, 0), 1.0 / 36.0),
    (11, 12, (1, 0, 1), 1.0 / 36.0),
    (13, 14, (1, 0, -1), 1.0 / 36.0),
    (15, 16, (0, 1, 1), 1.0 / 36.0),
    (17, 18, (0, 1, -1), 1.0 / 36.0),
)


def weights_of(fine):
    numer = 2 * fine + 9
    return numer // 16, (numer % 16) / 16.0


def col_table():
    table = np.zeros((128, 512), np.float32)
    for par in range(2):
        for fine in range(256):
            tile, inner = fine // 32, fine % 32
            low, frac = weights_of(inner)
            for off, weight in ((low, 1.0 - frac), (low + 1, frac)):
                if off == 0:
                    rim, j = 1, 0
                elif off == 5:
                    rim, j = 1, 3
                else:
                    rim, j = 0, off - 1
                table[par * 64 + rim * 32 + tile * 4 + j, par * 256 + fine] += weight
    return table


def row_table():
    table = np.zeros((32, 8), np.float32)
    for fine in range(32):
        low, frac = weights_of(fine)
        for off, weight in ((low, 1.0 - frac), (low + 1, frac)):
            place = 4 if off == 0 else off if off == 5 else off - 1
            table[fine, place] += 0.2 * weight
    return table


def force_table(lanes, width_y):
    width_x = 4 * lanes
    x = (np.arange(width_x) + 0.5) * (2.0 * math.pi / width_x)
    y = (np.arange(width_y) + 0.5) * (2.0 * math.pi / width_y)
    ax = np.tile(x.reshape(lanes, 4), (1, 2))[:, :, None]
    ay = y[None, None, :]
    full = (lanes, 8, width_y)
    return np.stack(
        [
            np.broadcast_to(np.cos(ax - 0.7), full),
            np.broadcast_to(np.sin(ay + 0.7), full),
            np.cos(ax + ay),
        ],
        axis=1,
    ).astype(np.float32)


def kernel(
    slabs, lanes,
    pop_hbm, gain_hbm, depth_hbm, phase_hbm, solute_hbm, ftab_hbm, ctab_hbm, rtab_hbm,
    vel, p_low, s_low, p1, s1, fine, hx_high, hy_high,
    pop, gain, depth, phase, solute, ftab, ctab, rtab,
    sums, xs, xr, zr, dr, vs, vr, v8, v8r, pk, wr, ex, hx, ey, hy,
    send, recv, local,
):
    gz, xy = lax.axis_index("gz"), lax.axis_index("xy")
    loads = []
    for src, dst in (
        (gain_hbm, gain), (ftab_hbm.at[xy], ftab), (pop_hbm, pop), (depth_hbm, depth),
        (phase_hbm, phase), (solute_hbm, solute), (ctab_hbm, ctab), (rtab_hbm, rtab),
    ):
        load = pltpu.make_async_copy(src, dst, local.at[len(loads)])
        load.start()
        loads.append(load)

    def at(dz, dx):
        return (lax.rem(gz + dz + slabs, slabs), lax.rem(xy + dx + lanes, lanes))

    peers = [(1, 0), (-1, 0), (0, 1), (0, -1), (1, 1), (1, -1), (-1, 1), (-1, -1)]
    peers += [(d, 0) for d in range(2, slabs - 1)]
    barrier = pltpu.get_barrier_semaphore()
    for peer in peers:
        pl.semaphore_signal(barrier, inc=1, device_id=at(*peer), device_id_type=MESH)

    count = [0]

    def remote(src, dst, where):
        i = count[0]
        count[0] += 1
        copy = pltpu.make_async_remote_copy(
            src_ref=src, dst_ref=dst, send_sem=send.at[i], recv_sem=recv.at[i],
            device_id=at(*where), device_id_type=MESH,
        )
        copy.start()
        return copy

    for load in loads[:3]:
        load.wait()
    rows32 = lax.broadcasted_iota(jnp.int32, (128, 32), 0) // 4
    cols32 = lax.broadcasted_iota(jnp.int32, (128, 32), 1)
    gain_col = jnp.sum(jnp.where(rows32 == cols32, gain[...], 0.0), axis=1, keepdims=True)
    shape = ftab[...]
    force = [
        jnp.broadcast_to(shape[c][None], (16, 8, 128)).reshape(128, 128) * gain_col
        for c in range(3)
    ]
    for c in range(3):
        vel[c] = force[c]

    def collide(i, carry):
        at_rows = pl.ds(pl.multiple_of(i * 8, 8), 8)
        f = [pop[q, at_rows, :] for q in range(19)]
        fc = [vel[c, at_rows, :] for c in range(3)]
        rho = f[0]
        mom = [0.5 * fc[0], 0.5 * fc[1], 0.5 * fc[2]]
        for a, b, e, _ in PAIRS:
            rho = rho + (f[a] + f[b])
            odd = f[a] - f[b]
            for c in range(3):
                if e[c] > 0:
                    mom[c] = mom[c] + odd
                elif e[c] < 0:
                    mom[c] = mom[c] - odd
        inv = 1.0 / rho
        u = [m * inv for m in mom]
        speed = u[0] * u[0] + u[1] * u[1] + u[2] * u[2]
        work = u[0] * fc[0] + u[1] * fc[1] + u[2] * fc[2]
        base = 1.25 * rho * (1.0 - 1.5 * speed) - 1.125 * work
        rho_a = 5.625 * rho
        rho_b = 3.75 * rho
        post = [None] * 19
        post[0] = -0.25 * f[0] + (1.0 / 3.0) * base

        def along(v, e):
            total = None
            for c in range(3):
                if e[c]:
                    term = v[c] if e[c] > 0 else -v[c]
                    total = term if total is None else total + term
            return total

        for a, b, e, w in PAIRS:
            cu, cf = along(u, e), along(fc, e)
            even = w * (base + cu * (rho_a * cu + 3.375 * cf))
            odd = w * (rho_b * cu + 1.125 * cf)
            post[a] = -0.25 * f[a] + (even + odd)
            post[b] = -0.25 * f[b] + (even - odd)

        def up(q):
            return pltpu.roll(post[q], 1, 1)

        def down(q):
            return pltpu.roll(post[q], 127, 1)

        def put(n, middle, plus, minus):
            a, b = up(plus), down(minus)
            sums[n, at_rows, :] = post[middle] + (a + b)
            sums[n + 1, at_rows, :] = a - b

        put(0, 1, 11, 13)
        sums[2, at_rows, :] = post[7]
        sums[3, at_rows, :] = post[9]
        put(4, 2, 14, 12)
        sums[6, at_rows, :] = post[10]
        sums[7, at_rows, :] = post[8]
        put(8, 3, 15, 17)
        put(10, 4, 18, 16)
        put(12, 0, 5, 6)
        return carry

    lax.fori_loop(0, 16, collide, 0)

    row = lax.broadcasted_iota(jnp.int32, (128, 128), 0)
    x_of = lax.rem(row, 4)
    plus_ids, minus_ids = (8, 9, 2, 6), (10, 11, 3, 7)

    def roll0(v, s):
        s = s % v.shape[0]
        return v if s == 0 else pltpu.roll(v, s, 0)

    def merge(values):
        out = values[-1]
        for m in range(len(values) - 1):
            out = jnp.where(x_of == m, values[m], out)
        return out

    xs[0] = merge([roll0(sums[i], m - 3) for m, i in enumerate(plus_ids)])
    xs[1] = merge([roll0(sums[i], m) for m, i in enumerate(minus_ids)])

    pl.semaphore_wait(barrier, len(peers))
    flow_copies = [
        remote(xs.at[0], xr.at[0], (0, 1)),
        remote(xs.at[1], xr.at[1], (0, -1)),
        remote(sums.at[pl.ds(0, 4), pl.ds(120, 8)], zr.at[0], (1, 0)),
        remote(sums.at[pl.ds(4, 4), pl.ds(0, 8)], zr.at[1], (-1, 0)),
        remote(sums.at[2, pl.ds(120, 8)], dr.at[0], (1, 1)),
        remote(sums.at[3, pl.ds(120, 8)], dr.at[1], (1, -1)),
        remote(sums.at[6, pl.ds(0, 8)], dr.at[2], (-1, 1)),
        remote(sums.at[7, pl.ds(0, 8)], dr.at[3], (-1, -1)),
    ]

    for load in loads[3:]:
        load.wait()
    lane = lax.broadcasted_iota(jnp.int32, (32, 128), 1)

    def edges(k, carry):
        first, last = carry
        for n, ref in enumerate((phase, solute)):
            ex[0, 0, n, pl.ds(k, 1), :] = ref[k, 31:32, :]
            ex[0, 1, n, pl.ds(k, 1), :] = ref[k, 0:1, :]
            here = lane == k + 32 * n
            last = jnp.where(here, ref[k, :, 255:256], last)
            first = jnp.where(here, ref[k, :, 0:1], first)
        return first, last

    nothing = jnp.zeros((32, 128), F32)
    first, last = lax.fori_loop(0, 32, edges, (nothing, nothing))
    ey[0, 0] = last
    ey[0, 1] = first

    band_copies = [
        remote(ex.at[0, 0], hx.at[0, 0], (0, 1)),
        remote(ex.at[0, 1], hx.at[0, 1], (0, -1)),
        remote(ey.at[0, 0], hy.at[0, 0], (1, 0)),
        remote(ey.at[0, 1], hy.at[0, 1], (-1, 0)),
    ]
    for copy in flow_copies:
        copy.wait()

    sub = lax.broadcasted_iota(jnp.int32, (8, 128), 0)

    def shift_x(i, sign):
        if sign > 0:
            m = plus_ids.index(i)
            return jnp.where(x_of == 0, roll0(xr[0], -m), roll0(sums[i], 1))
        m = minus_ids.index(i)
        return jnp.where(x_of == 3, roll0(xr[1], 3 - m), roll0(sums[i], -1))

    def shift_z(value, sign, block):
        moved = roll0(value, 4 * sign)
        if sign > 0:
            return jnp.concatenate([jnp.where(sub < 4, block, moved[:8]), moved[8:]], axis=0)
        return jnp.concatenate([moved[:120], jnp.where(sub >= 4, block, moved[120:])], axis=0)

    rho = sums[12]
    my = sums[13]
    a = shift_x(8, 1)
    b = shift_x(10, -1)
    rho = rho + (a + b)
    mx = a - b
    my = my + (shift_x(9, 1) + shift_x(11, -1))
    a = shift_z(sums[0], 1, roll0(zr[0, 0], 4))
    b = shift_z(sums[4], -1, roll0(zr[1, 0], 4))
    rho = rho + (a + b)
    mz = a - b
    my = my + shift_z(sums[1], 1, roll0(zr[0, 1], 4))
    my = my + shift_z(sums[5], -1, roll0(zr[1, 1], 4))
    a = shift_z(shift_x(2, 1), 1, jnp.where(sub == 0, roll0(dr[0], 1), roll0(zr[0, 2], 5)))
    b = shift_z(shift_x(7, -1), -1, jnp.where(sub == 7, roll0(dr[3], 7), roll0(zr[1, 3], 3)))
    rho = rho + (a + b)
    mz = mz + (a - b)
    mx = mx + (a - b)
    a = shift_z(shift_x(3, -1), 1, jnp.where(sub == 3, roll0(dr[1], 7), roll0(zr[0, 3], 3)))
    b = shift_z(shift_x(6, 1), -1, jnp.where(sub == 4, roll0(dr[2], 1), roll0(zr[1, 2], 5)))
    rho = rho + (a + b)
    mz = mz + (a - b)
    mx = mx - (a - b)
    inv = 1.0 / rho
    v = [(m + 0.5 * vel[c]) * inv for c, m in enumerate((mz, mx, my))]
    for c in range(3):
        vel[c] = v[c]
    vs[0] = merge([roll0(v[c], c - 3) for c in range(3)])
    vs[1] = merge([roll0(v[c], c) for c in range(3)])
    rim_copies = [
        remote(vs.at[0], vr.at[0], (0, 1)),
        remote(vs.at[1], vr.at[1], (0, -1)),
    ]
    for copy in rim_copies:
        copy.wait()

    sub128 = lax.rem(row, 8)
    lane128 = lax.broadcasted_iota(jnp.int32, (128, 128), 1)
    lane_in = lax.rem(lane128, 4)
    for c in range(3):
        own = vel[c]
        for par in range(2):
            block = jnp.where(
                sub128 == 4,
                roll0(vr[0], 4 - c - 4 * par),
                jnp.where(sub128 == 5, roll0(vr[1], 5 - c - 4 * par), roll0(own, -4 * par)),
            )
            v8[c, par] = block.reshape(16, 8, 128)
            side = jnp.where(lane_in == 0, pltpu.roll(block, 1, 1), pltpu.roll(block, 127, 1))
            v8r[c, par] = side.reshape(16, 8, 128)

    lane8 = lax.broadcasted_iota(jnp.int32, (8, 128), 1)
    tile_of = lane8 // 4
    group_of = lane8 // 32
    tiles_z = 8 * slabs
    none8 = jnp.zeros((8, 128), F32)

    def gather(tile, carry):
        here_z = depth[0, tile]
        prev_z = jnp.where(here_z == 0, tiles_z - 1, here_z - 1)
        next_z = jnp.where(here_z == tiles_z - 1, 0, here_z + 1)
        masks, places = [], []
        for at_tile in (prev_z, here_z, next_z):
            masks.append(tile_of == jnp.where((at_tile >> 3) == gz, tile, -1))
            places.append((at_tile & 7) * 2)
        picks = [(0, 1, places[0] + 1)]
        picks += [(1, i % 2, places[1] + i // 2) for i in range(4)]
        picks += [(2, 0, places[2])]
        out = []
        for c in range(3):
            for dz, (m, par, half) in enumerate(picks):
                out.append(jnp.where(masks[m], v8[c, par, half], carry[12 * c + 2 * dz]))
                out.append(jnp.where(masks[m], v8r[c, par, half], carry[12 * c + 2 * dz + 1]))
        return tuple(out)

    items = lax.fori_loop(0, 8 * slabs, gather, (none8,) * 36)
    for c in range(3):
        for target in range(slabs):
            for m in range(3):
                out = none8
                for g in range(4):
                    item = items[12 * c + 4 * m + g]
                    s = (32 * (g - target)) % 128
                    moved = item if s == 0 else pltpu.roll(item, s, 1)
                    out = jnp.where(group_of == g, moved, out)
                pk[target, 3 * c + m] = out

    window_copies = [
        remote(pk.at[lax.rem(gz + d, slabs)], wr.at[d - 1], (d, 0)) for d in range(1, slabs)
    ]
    windows = pk[gz]
    for d, copy in enumerate(window_copies):
        copy.wait()
        windows = windows + wr[d]
    wide = jnp.dot(
        windows.reshape(72, 128), ctab[...],
        precision=lax.Precision.HIGHEST, preferred_element_type=F32,
    )
    for c in range(3):
        for dz in range(6):
            at_row = (3 * c + dz // 2) * 8
            at_col = (dz % 2) * 256
            fine[c, dz] = jnp.dot(
                rtab[...], wide[at_row:at_row + 8, at_col:at_col + 256],
                precision=lax.Precision.HIGHEST, preferred_element_type=F32,
            )

    def keep_edges(k, results, carry):
        last, first = carry
        for n, (left, right) in enumerate(results):
            ex[1, 0, n, pl.ds(k, 1), :] = jnp.concatenate([left[31:32], right[31:32]], axis=1)
            ex[1, 1, n, pl.ds(k, 1), :] = jnp.concatenate([left[0:1], right[0:1]], axis=1)
            here = lane == k + 32 * n
            last = jnp.where(here, right[:, 127:128], last)
            first = jnp.where(here, left[:, 0:1], first)
        return last, first

    for copy in band_copies:
        copy.wait()
    sides = (hy[0, 0], hy[0, 1])
    halves = []
    for half in range(2):
        ks = slice(16 * half, 16 * half + 16)

        def first_step(k, carry):
            results = plane(k, (phase, solute), fine, hx.at[0], k, carry[:2])
            for dst, (left, right) in zip((p1, s1), results):
                dst[k, :, :128] = left
                dst[k, :, 128:] = right
            return next_sides(carry[:2]) + keep_edges(k, results, carry[2:])

        *sides, last, first = lax.fori_loop(
            16 * half, 16 * half + 16, first_step, (*sides, nothing, nothing)
        )
        ey[1 + half, 0] = last
        ey[1 + half, 1] = first
        halves.append([
            remote(ex.at[1, 0, :, ks], hx.at[1, 0, :, ks], (0, 1)),
            remote(ex.at[1, 1, :, ks], hx.at[1, 1, :, ks], (0, -1)),
            remote(ey.at[1 + half, 0], hy.at[1 + half, 0], (1, 0)),
            remote(ey.at[1 + half, 1], hy.at[1 + half, 1], (-1, 0)),
        ])
    for copy in halves[0]:
        copy.wait()

    def second_step(k, carry):
        results = plane(k, (p1, s1), fine, hx.at[1], k, carry)
        for dst, (left, right) in zip((p_low, s_low), results):
            dst[k, :, :128] = left
            dst[k, :, 128:] = right
        return next_sides(carry)

    lax.fori_loop(0, 16, second_step, (hy[1, 0], hy[1, 1]))
    for copy in halves[1]:
        copy.wait()
    hx_high[...] = hx[1, :, :, 16:32]
    hy_high[...] = hy[2]


def next_sides(sides):
    return tuple(pltpu.roll(v, 127, 1) for v in sides)


def plane(k, src, fine, rows, row_at, sides):
    sub = lax.broadcasted_iota(jnp.int32, (32, 128), 0)
    lane = lax.broadcasted_iota(jnp.int32, (32, 128), 1)
    before, after = sides
    low = (2 * k + 9) >> 4
    frac = ((2 * k + 9) & 15).astype(F32) * (1.0 / 16.0)
    above, below = jnp.minimum(k + 1, 31), jnp.maximum(k - 1, 0)
    along_y = []
    for n, ref in enumerate(src):
        left, right = ref[k, :, :128], ref[k, :, 128:]
        left_up, right_up = pltpu.roll(left, 127, 1), pltpu.roll(right, 127, 1)
        left_dn, right_dn = pltpu.roll(left, 1, 1), pltpu.roll(right, 1, 1)
        edge_up, edge_dn = after[:, 32 * n:32 * n + 1], before[:, 32 * n:32 * n + 1]
        along_y.append((
            (jnp.where(lane == 127, right_up, left_up), jnp.where(lane == 0, edge_dn, left_dn)),
            (jnp.where(lane == 127, edge_up, right_up), jnp.where(lane == 0, left_dn, right_dn)),
        ))
    out_p, out_s = [], []
    for half in range(2):
        cols = slice(128 * half, 128 * half + 128)
        flow = []
        for c in range(3):
            lower = fine[c, low, :, cols]
            flow.append(lower + frac * (fine[c, low + 1, :, cols] - lower))
        terms = []
        for n, ref in enumerate(src):
            mid = ref[k, :, cols]
            zu, zd = ref[above, :, cols], ref[below, :, cols]
            row_up = rows[1, n, pl.ds(row_at, 1), :][:, cols]
            row_dn = rows[0, n, pl.ds(row_at, 1), :][:, cols]
            xu = jnp.where(sub == 31, row_up, pltpu.roll(mid, 31, 0))
            xd = jnp.where(sub == 0, row_dn, pltpu.roll(mid, 1, 0))
            yu, yd = along_y[n][half]
            drift = flow[0] * (zu - zd) + flow[1] * (xu - xd) + flow[2] * (yu - yd)
            terms.append((mid, zu + zd, (xu + xd) + (yu + yd), drift))
        p, zz, side, drift = terms[0]
        s, zz_s, side_s, drift_s = terms[1]
        drive = p * (1.0 - p) * (0.4 * p + 0.2 * s - 0.4)
        change = 0.15 * zz + 0.1 * side - 0.7 * p - drift + drive
        out_p.append(p + change)
        out_s.append(0.4 * s + 0.1 * (zz_s + side_s) - drift_s + 0.85 * s * change)
    return out_p, out_s


def finish(
    vel, p_low, s_low, p1, s1, fine, hx_high, hy_high,
    vel_out, p_out, s_out, p_high, s_high, sems,
):
    copies = [
        pltpu.make_async_copy(vel, vel_out, sems.at[0]),
        pltpu.make_async_copy(p_low, p_out.at[0:16], sems.at[1]),
        pltpu.make_async_copy(s_low, s_out.at[0:16], sems.at[2]),
    ]
    for copy in copies:
        copy.start()
    sides = tuple(pltpu.roll(hy_high[i], 112, 1) for i in range(2))
    for part in range(2):

        def step(k, carry):
            results = plane(k + 16, (p1, s1), fine, hx_high, k, carry)
            for dst, (left, right) in zip((p_high, s_high), results):
                dst[k, :, :128] = left
                dst[k, :, 128:] = right
            return next_sides(carry)

        sides = lax.fori_loop(8 * part, 8 * part + 8, step, sides)
        here = slice(8 * part, 8 * part + 8)
        there = slice(16 + 8 * part, 24 + 8 * part)
        for n, (src, dst) in enumerate(((p_high, p_out), (s_high, s_out))):
            copy = pltpu.make_async_copy(
                src.at[here], dst.at[there], sems.at[3 + 2 * part + n]
            )
            copy.start()
            copies.append(copy)
    for copy in copies:
        copy.wait()


def body(slabs, lanes, populations, field_gain, front_depth, phase, solute):
    depth_here, rows_here, cols = populations.shape[1:]
    pops = populations.reshape(19, depth_here * rows_here, cols)
    vmem = pl.BlockSpec(memory_space=pltpu.VMEM)
    anywhere = pl.BlockSpec(memory_space=pltpu.HBM)
    copies = 8 + 4 + 2 + (slabs - 1) + 8
    passed = pl.pallas_call(
        functools.partial(kernel, slabs, lanes),
        out_shape=(
            jax.ShapeDtypeStruct((3, 128, 128), F32),
            jax.ShapeDtypeStruct((16, 32, 256), F32),
            jax.ShapeDtypeStruct((16, 32, 256), F32),
            jax.ShapeDtypeStruct(phase.shape, F32),
            jax.ShapeDtypeStruct(solute.shape, F32),
            jax.ShapeDtypeStruct((3, 6, 32, 256), F32),
            jax.ShapeDtypeStruct((2, 2, 16, 256), F32),
            jax.ShapeDtypeStruct((2, 32, 128), F32),
        ),
        in_specs=[anywhere] * 8,
        out_specs=(vmem,) * 8,
        scratch_shapes=[
            pltpu.VMEM(pops.shape, F32),
            pltpu.VMEM((1, depth_here), F32),
            pltpu.SMEM(front_depth.shape, jnp.int32),
            pltpu.VMEM(phase.shape, F32),
            pltpu.VMEM(solute.shape, F32),
            pltpu.VMEM((3, 8, cols), F32),
            pltpu.VMEM((128, 512), F32),
            pltpu.VMEM((32, 8), F32),
            pltpu.VMEM((14, 128, 128), F32),
            pltpu.VMEM((2, 128, 128), F32),
            pltpu.VMEM((2, 128, 128), F32),
            pltpu.VMEM((2, 4, 8, 128), F32),
            pltpu.VMEM((4, 8, 128), F32),
            pltpu.VMEM((2, 128, 128), F32),
            pltpu.VMEM((2, 128, 128), F32),
            pltpu.VMEM((3, 2, 16, 8, 128), F32),
            pltpu.VMEM((3, 2, 16, 8, 128), F32),
            pltpu.VMEM((slabs, 9, 8, 128), F32),
            pltpu.VMEM((slabs - 1, 9, 8, 128), F32),
            pltpu.VMEM((2, 2, 2, 32, 256), F32),
            pltpu.VMEM((2, 2, 2, 32, 256), F32),
            pltpu.VMEM((3, 2, 32, 128), F32),
            pltpu.VMEM((3, 2, 32, 128), F32),
            pltpu.SemaphoreType.DMA((copies,)),
            pltpu.SemaphoreType.DMA((copies,)),
            pltpu.SemaphoreType.DMA((8,)),
        ],
        compiler_params=pltpu.CompilerParams(
            collective_id=0, has_side_effects=True, vmem_limit_bytes=24 * 2**20
        ),
    )(
        pops,
        field_gain.reshape(1, depth_here),
        front_depth,
        phase,
        solute,
        jnp.asarray(force_table(lanes, cols)),
        jnp.asarray(col_table()),
        jnp.asarray(row_table()),
    )
    velocity, phase_next, solute_next = pl.pallas_call(
        finish,
        out_shape=(
            jax.ShapeDtypeStruct((3, 128, 128), F32),
            jax.ShapeDtypeStruct(phase.shape, F32),
            jax.ShapeDtypeStruct(solute.shape, F32),
        ),
        in_specs=[vmem] * 8,
        out_specs=(anywhere,) * 3,
        scratch_shapes=[
            pltpu.VMEM((16, 32, 256), F32),
            pltpu.VMEM((16, 32, 256), F32),
            pltpu.SemaphoreType.DMA((7,)),
        ],
        compiler_params=pltpu.CompilerParams(vmem_limit_bytes=16 * 2**20),
    )(*passed)
    return velocity.reshape(3, depth_here, rows_here, cols), phase_next, solute_next


def solution(mesh):
    return jax.shard_map(
        functools.partial(body, mesh.shape["gz"], mesh.shape["xy"]),
        mesh=mesh,
        in_specs=(
            P(None, "gz", "xy", None),
            P("gz"),
            P("xy", None),
            P(None, "xy", "gz"),
            P(None, "xy", "gz"),
        ),
        out_specs=(P(None, "gz", "xy", None), P(None, "xy", "gz"), P(None, "xy", "gz")),
        check_vma=False,
    )
```

```python
import functools
import math

import jax
import jax.numpy as jnp
import numpy as np
from jax import lax
from jax.experimental import pallas as pl
from jax.experimental.pallas import tpu as pltpu
from jax.sharding import PartitionSpec as P

MESH = pl.DeviceIdType.MESH
F32 = jnp.float32

PAIRS = (
    (1, 2, (1, 0, 0), 1.0 / 18.0),
    (3, 4, (0, 1, 0), 1.0 / 18.0),
    (5, 6, (0, 0, 1), 1.0 / 18.0),
    (7, 8, (1, 1, 0), 1.0 / 36.0),
    (9, 10, (1, -1, 0), 1.0 / 36.0),
    (11, 12, (1, 0, 1), 1.0 / 36.0),
    (13, 14, (1, 0, -1), 1.0 / 36.0),
    (15, 16, (0, 1, 1), 1.0 / 36.0),
    (17, 18, (0, 1, -1), 1.0 / 36.0),
)


def weights_of(fine):
    numer = 2 * fine + 9
    return numer // 16, (numer % 16) / 16.0


def col_table():
    table = np.zeros((128, 512), np.float32)
    for par in range(2):
        for fine in range(256):
            tile, inner = fine // 32, fine % 32
            low, frac = weights_of(inner)
            for off, weight in ((low, 1.0 - frac), (low + 1, frac)):
                if off == 0:
                    rim, j = 1, 0
                elif off == 5:
                    rim, j = 1, 3
                else:
                    rim, j = 0, off - 1
                table[par * 64 + rim * 32 + tile * 4 + j, par * 256 + fine] += weight
    return table


def row_table():
    table = np.zeros((32, 8), np.float32)
    for fine in range(32):
        low, frac = weights_of(fine)
        for off, weight in ((low, 1.0 - frac), (low + 1, frac)):
            place = 4 if off == 0 else off if off == 5 else off - 1
            table[fine, place] += 0.2 * weight
    return table


def force_table(lanes, width_y):
    width_x = 4 * lanes
    x = (np.arange(width_x) + 0.5) * (2.0 * math.pi / width_x)
    y = (np.arange(width_y) + 0.5) * (2.0 * math.pi / width_y)
    ax = np.tile(x.reshape(lanes, 4), (1, 2))[:, :, None]
    ay = y[None, None, :]
    full = (lanes, 8, width_y)
    return np.stack(
        [
            np.broadcast_to(np.cos(ax - 0.7), full),
            np.broadcast_to(np.sin(ay + 0.7), full),
            np.cos(ax + ay),
        ],
        axis=1,
    ).astype(np.float32)


def kernel(
    slabs, lanes,
    pop_hbm, gain_hbm, depth_hbm, phase_hbm, solute_hbm, ftab_hbm, ctab_hbm, rtab_hbm,
    vel, p_low, s_low, p1, s1, fine, hx_high, hy_high,
    pop, gain, depth, phase, solute, ftab, ctab, rtab,
    sums, xs, xr, zr, dr, vs, vr, v8, v8r, pk, wr, ex, hx, ey, hy,
    send, recv, local,
):
    gz, xy = lax.axis_index("gz"), lax.axis_index("xy")
    loads = []
    for src, dst in (
        (gain_hbm, gain), (ftab_hbm.at[xy], ftab), (pop_hbm, pop), (depth_hbm, depth),
        (phase_hbm, phase), (solute_hbm, solute), (ctab_hbm, ctab), (rtab_hbm, rtab),
    ):
        load = pltpu.make_async_copy(src, dst, local.at[len(loads)])
        load.start()
        loads.append(load)

    def at(dz, dx):
        return (lax.rem(gz + dz + slabs, slabs), lax.rem(xy + dx + lanes, lanes))

    peers = [(1, 0), (-1, 0), (0, 1), (0, -1), (1, 1), (1, -1), (-1, 1), (-1, -1)]
    peers += [(d, 0) for d in range(2, slabs - 1)]
    barrier = pltpu.get_barrier_semaphore()
    for peer in peers:
        pl.semaphore_signal(barrier, inc=1, device_id=at(*peer), device_id_type=MESH)

    count = [0]

    def remote(src, dst, where):
        i = count[0]
        count[0] += 1
        copy = pltpu.make_async_remote_copy(
            src_ref=src, dst_ref=dst, send_sem=send.at[i], recv_sem=recv.at[i],
            device_id=at(*where), device_id_type=MESH,
        )
        copy.start()
        return copy

    for load in loads[:3]:
        load.wait()
    rows32 = lax.broadcasted_iota(jnp.int32, (128, 32), 0) // 4
    cols32 = lax.broadcasted_iota(jnp.int32, (128, 32), 1)
    gain_col = jnp.sum(jnp.where(rows32 == cols32, gain[...], 0.0), axis=1, keepdims=True)
    shape = ftab[...]
    force = [
        jnp.broadcast_to(shape[c][None], (16, 8, 128)).reshape(128, 128) * gain_col
        for c in range(3)
    ]
    for c in range(3):
        vel[c] = force[c]

    def collide(i, carry):
        at_rows = pl.ds(pl.multiple_of(i * 8, 8), 8)
        f = [pop[q, at_rows, :] for q in range(19)]
        fc = [vel[c, at_rows, :] for c in range(3)]
        rho = f[0]
        mom = [0.5 * fc[0], 0.5 * fc[1], 0.5 * fc[2]]
        for a, b, e, _ in PAIRS:
            rho = rho + (f[a] + f[b])
            odd = f[a] - f[b]
            for c in range(3):
                if e[c] > 0:
                    mom[c] = mom[c] + odd
                elif e[c] < 0:
                    mom[c] = mom[c] - odd
        inv = 1.0 / rho
        u = [m * inv for m in mom]
        speed = u[0] * u[0] + u[1] * u[1] + u[2] * u[2]
        work = u[0] * fc[0] + u[1] * fc[1] + u[2] * fc[2]
        base = 1.25 * rho * (1.0 - 1.5 * speed) - 1.125 * work
        rho_a = 5.625 * rho
        rho_b = 3.75 * rho
        post = [None] * 19
        post[0] = -0.25 * f[0] + (1.0 / 3.0) * base

        def along(v, e):
            total = None
            for c in range(3):
                if e[c]:
                    term = v[c] if e[c] > 0 else -v[c]
                    total = term if total is None else total + term
            return total

        for a, b, e, w in PAIRS:
            cu, cf = along(u, e), along(fc, e)
            even = w * (base + cu * (rho_a * cu + 3.375 * cf))
            odd = w * (rho_b * cu + 1.125 * cf)
            post[a] = -0.25 * f[a] + (even + odd)
            post[b] = -0.25 * f[b] + (even - odd)

        def up(q):
            return pltpu.roll(post[q], 1, 1)

        def down(q):
            return pltpu.roll(post[q], 127, 1)

        def put(n, middle, plus, minus):
            a, b = up(plus), down(minus)
            sums[n, at_rows, :] = post[middle] + (a + b)
            sums[n + 1, at_rows, :] = a - b

        put(0, 1, 11, 13)
        sums[2, at_rows, :] = post[7]
        sums[3, at_rows, :] = post[9]
        put(4, 2, 14, 12)
        sums[6, at_rows, :] = post[10]
        sums[7, at_rows, :] = post[8]
        put(8, 3, 15, 17)
        put(10, 4, 18, 16)
        put(12, 0, 5, 6)
        return carry

    lax.fori_loop(0, 16, collide, 0)

    row = lax.broadcasted_iota(jnp.int32, (128, 128), 0)
    x_of = lax.rem(row, 4)
    plus_ids, minus_ids = (8, 9, 2, 6), (10, 11, 3, 7)

    def roll0(v, s):
        s = s % v.shape[0]
        return v if s == 0 else pltpu.roll(v, s, 0)

    def merge(values):
        out = values[-1]
        for m in range(len(values) - 1):
            out = jnp.where(x_of == m, values[m], out)
        return out

    xs[0] = merge([roll0(sums[i], m - 3) for m, i in enumerate(plus_ids)])
    xs[1] = merge([roll0(sums[i], m) for m, i in enumerate(minus_ids)])

    pl.semaphore_wait(barrier, len(peers))
    flow_copies = [
        remote(xs.at[0], xr.at[0], (0, 1)),
        remote(xs.at[1], xr.at[1], (0, -1)),
        remote(sums.at[pl.ds(0, 4), pl.ds(120, 8)], zr.at[0], (1, 0)),
        remote(sums.at[pl.ds(4, 4), pl.ds(0, 8)], zr.at[1], (-1, 0)),
        remote(sums.at[2, pl.ds(120, 8)], dr.at[0], (1, 1)),
        remote(sums.at[3, pl.ds(120, 8)], dr.at[1], (1, -1)),
        remote(sums.at[6, pl.ds(0, 8)], dr.at[2], (-1, 1)),
        remote(sums.at[7, pl.ds(0, 8)], dr.at[3], (-1, -1)),
    ]

    for load in loads[3:]:
        load.wait()
    lane = lax.broadcasted_iota(jnp.int32, (32, 128), 1)

    def edges(k, carry):
        first, last = carry
        for n, ref in enumerate((phase, solute)):
            ex[0, 0, n, pl.ds(k, 1), :] = ref[k, 31:32, :]
            ex[0, 1, n, pl.ds(k, 1), :] = ref[k, 0:1, :]
            here = lane == k + 32 * n
            last = jnp.where(here, ref[k, :, 255:256], last)
            first = jnp.where(here, ref[k, :, 0:1], first)
        return first, last

    nothing = jnp.zeros((32, 128), F32)
    first, last = lax.fori_loop(0, 32, edges, (nothing, nothing))
    ey[0, 0] = last
    ey[0, 1] = first

    band_copies = [
        remote(ex.at[0, 0], hx.at[0, 0], (0, 1)),
        remote(ex.at[0, 1], hx.at[0, 1], (0, -1)),
        remote(ey.at[0, 0], hy.at[0, 0], (1, 0)),
        remote(ey.at[0, 1], hy.at[0, 1], (-1, 0)),
    ]
    for copy in flow_copies:
        copy.wait()

    sub = lax.broadcasted_iota(jnp.int32, (8, 128), 0)

    def shift_x(i, sign):
        if sign > 0:
            m = plus_ids.index(i)
            return jnp.where(x_of == 0, roll0(xr[0], -m), roll0(sums[i], 1))
        m = minus_ids.index(i)
        return jnp.where(x_of == 3, roll0(xr[1], 3 - m), roll0(sums[i], -1))

    def shift_z(value, sign, block):
        moved = roll0(value, 4 * sign)
        if sign > 0:
            return jnp.concatenate([jnp.where(sub < 4, block, moved[:8]), moved[8:]], axis=0)
        return jnp.concatenate([moved[:120], jnp.where(sub >= 4, block, moved[120:])], axis=0)

    rho = sums[12]
    my = sums[13]
    a = shift_x(8, 1)
    b = shift_x(10, -1)
    rho = rho + (a + b)
    mx = a - b
    my = my + (shift_x(9, 1) + shift_x(11, -1))
    a = shift_z(sums[0], 1, roll0(zr[0, 0], 4))
    b = shift_z(sums[4], -1, roll0(zr[1, 0], 4))
    rho = rho + (a + b)
    mz = a - b
    my = my + shift_z(sums[1], 1, roll0(zr[0, 1], 4))
    my = my + shift_z(sums[5], -1, roll0(zr[1, 1], 4))
    a = shift_z(shift_x(2, 1), 1, jnp.where(sub == 0, roll0(dr[0], 1), roll0(zr[0, 2], 5)))
    b = shift_z(shift_x(7, -1), -1, jnp.where(sub == 7, roll0(dr[3], 7), roll0(zr[1, 3], 3)))
    rho = rho + (a + b)
    mz = mz + (a - b)
    mx = mx + (a - b)
    a = shift_z(shift_x(3, -1), 1, jnp.where(sub == 3, roll0(dr[1], 7), roll0(zr[0, 3], 3)))
    b = shift_z(shift_x(6, 1), -1, jnp.where(sub == 4, roll0(dr[2], 1), roll0(zr[1, 2], 5)))
    rho = rho + (a + b)
    mz = mz + (a - b)
    mx = mx - (a - b)
    inv = 1.0 / rho
    v = [(m + 0.5 * vel[c]) * inv for c, m in enumerate((mz, mx, my))]
    for c in range(3):
        vel[c] = v[c]
    vs[0] = merge([roll0(v[c], c - 3) for c in range(3)])
    vs[1] = merge([roll0(v[c], c) for c in range(3)])
    rim_copies = [
        remote(vs.at[0], vr.at[0], (0, 1)),
        remote(vs.at[1], vr.at[1], (0, -1)),
    ]
    for copy in rim_copies:
        copy.wait()

    sub128 = lax.rem(row, 8)
    lane128 = lax.broadcasted_iota(jnp.int32, (128, 128), 1)
    lane_in = lax.rem(lane128, 4)
    for c in range(3):
        own = vel[c]
        for par in range(2):
            block = jnp.where(
                sub128 == 4,
                roll0(vr[0], 4 - c - 4 * par),
                jnp.where(sub128 == 5, roll0(vr[1], 5 - c - 4 * par), roll0(own, -4 * par)),
            )
            v8[c, par] = block.reshape(16, 8, 128)
            side = jnp.where(lane_in == 0, pltpu.roll(block, 1, 1), pltpu.roll(block, 127, 1))
            v8r[c, par] = side.reshape(16, 8, 128)

    lane8 = lax.broadcasted_iota(jnp.int32, (8, 128), 1)
    tile_of = lane8 // 4
    group_of = lane8 // 32
    tiles_z = 8 * slabs
    none8 = jnp.zeros((8, 128), F32)

    def gather(tile, carry):
        here_z = depth[0, tile]
        prev_z = jnp.where(here_z == 0, tiles_z - 1, here_z - 1)
        next_z = jnp.where(here_z == tiles_z - 1, 0, here_z + 1)
        masks, places = [], []
        for at_tile in (prev_z, here_z, next_z):
            masks.append(tile_of == jnp.where((at_tile >> 3) == gz, tile, -1))
            places.append((at_tile & 7) * 2)
        picks = [(0, 1, places[0] + 1)]
        picks += [(1, i % 2, places[1] + i // 2) for i in range(4)]
        picks += [(2, 0, places[2])]
        out = []
        for c in range(3):
            for dz, (m, par, half) in enumerate(picks):
                out.append(jnp.where(masks[m], v8[c, par, half], carry[12 * c + 2 * dz]))
                out.append(jnp.where(masks[m], v8r[c, par, half], carry[12 * c + 2 * dz + 1]))
        return tuple(out)

    items = lax.fori_loop(0, 8 * slabs, gather, (none8,) * 36)
    for c in range(3):
        for target in range(slabs):
            for m in range(3):
                out = none8
                for g in range(4):
                    item = items[12 * c + 4 * m + g]
                    s = (32 * (g - target)) % 128
                    moved = item if s == 0 else pltpu.roll(item, s, 1)
                    out = jnp.where(group_of == g, moved, out)
                pk[target, 3 * c + m] = out

    window_copies = [
        remote(pk.at[lax.rem(gz + d, slabs)], wr.at[d - 1], (d, 0)) for d in range(1, slabs)
    ]
    windows = pk[gz]
    for d, copy in enumerate(window_copies):
        copy.wait()
        windows = windows + wr[d]
    wide = jnp.dot(
        windows.reshape(72, 128), ctab[...],
        precision=lax.Precision.HIGHEST, preferred_element_type=F32,
    )
    for c in range(3):
        for dz in range(6):
            at_row = (3 * c + dz // 2) * 8
            at_col = (dz % 2) * 256
            fine[c, dz] = jnp.dot(
                rtab[...], wide[at_row:at_row + 8, at_col:at_col + 256],
                precision=lax.Precision.HIGHEST, preferred_element_type=F32,
            )

    def keep_edges(k, results, carry):
        last, first = carry
        for n, (left, right) in enumerate(results):
            ex[1, 0, n, pl.ds(k, 1), :] = jnp.concatenate([left[31:32], right[31:32]], axis=1)
            ex[1, 1, n, pl.ds(k, 1), :] = jnp.concatenate([left[0:1], right[0:1]], axis=1)
            here = lane == k + 32 * n
            last = jnp.where(here, right[:, 127:128], last)
            first = jnp.where(here, left[:, 0:1], first)
        return last, first

    for copy in band_copies:
        copy.wait()
    sides = (hy[0, 0], hy[0, 1])
    halves = []
    for half in range(2):
        ks = slice(16 * half, 16 * half + 16)

        def first_step(k, carry):
            results = plane(k, (phase, solute), fine, hx.at[0], k, carry[:2])
            for dst, (left, right) in zip((p1, s1), results):
                dst[k, :, :128] = left
                dst[k, :, 128:] = right
            return next_sides(carry[:2]) + keep_edges(k, results, carry[2:])

        *sides, last, first = lax.fori_loop(
            16 * half, 16 * half + 16, first_step, (*sides, nothing, nothing)
        )
        ey[1 + half, 0] = last
        ey[1 + half, 1] = first
        halves.append([
            remote(ex.at[1, 0, :, ks], hx.at[1, 0, :, ks], (0, 1)),
            remote(ex.at[1, 1, :, ks], hx.at[1, 1, :, ks], (0, -1)),
            remote(ey.at[1 + half, 0], hy.at[1 + half, 0], (1, 0)),
            remote(ey.at[1 + half, 1], hy.at[1 + half, 1], (-1, 0)),
        ])
    for copy in halves[0]:
        copy.wait()

    def second_step(k, carry):
        results = plane(k, (p1, s1), fine, hx.at[1], k, carry)
        for dst, (left, right) in zip((p_low, s_low), results):
            dst[k, :, :128] = left
            dst[k, :, 128:] = right
        return next_sides(carry)

    lax.fori_loop(0, 16, second_step, (hy[1, 0], hy[1, 1]))
    for copy in halves[1]:
        copy.wait()
    hx_high[...] = hx[1, :, :, 16:32]
    hy_high[...] = hy[2]


def next_sides(sides):
    return tuple(pltpu.roll(v, 127, 1) for v in sides)


def plane(k, src, fine, rows, row_at, sides):
    sub = lax.broadcasted_iota(jnp.int32, (32, 128), 0)
    lane = lax.broadcasted_iota(jnp.int32, (32, 128), 1)
    before, after = sides
    low = (2 * k + 9) >> 4
    frac = ((2 * k + 9) & 15).astype(F32) * (1.0 / 16.0)
    above, below = jnp.minimum(k + 1, 31), jnp.maximum(k - 1, 0)
    along_y = []
    for n, ref in enumerate(src):
        left, right = ref[k, :, :128], ref[k, :, 128:]
        left_up, right_up = pltpu.roll(left, 127, 1), pltpu.roll(right, 127, 1)
        left_dn, right_dn = pltpu.roll(left, 1, 1), pltpu.roll(right, 1, 1)
        edge_up, edge_dn = after[:, 32 * n:32 * n + 1], before[:, 32 * n:32 * n + 1]
        along_y.append((
            (jnp.where(lane == 127, right_up, left_up), jnp.where(lane == 0, edge_dn, left_dn)),
            (jnp.where(lane == 127, edge_up, right_up), jnp.where(lane == 0, left_dn, right_dn)),
        ))
    out_p, out_s = [], []
    for half in range(2):
        cols = slice(128 * half, 128 * half + 128)
        flow = []
        for c in range(3):
            lower = fine[c, low, :, cols]
            flow.append(lower + frac * (fine[c, low + 1, :, cols] - lower))
        terms = []
        for n, ref in enumerate(src):
            mid = ref[k, :, cols]
            zu, zd = ref[above, :, cols], ref[below, :, cols]
            row_up = rows[1, n, pl.ds(row_at, 1), :][:, cols]
            row_dn = rows[0, n, pl.ds(row_at, 1), :][:, cols]
            xu = jnp.where(sub == 31, row_up, pltpu.roll(mid, 31, 0))
            xd = jnp.where(sub == 0, row_dn, pltpu.roll(mid, 1, 0))
            yu, yd = along_y[n][half]
            drift = flow[0] * (zu - zd) + flow[1] * (xu - xd) + flow[2] * (yu - yd)
            terms.append((mid, zu + zd, (xu + xd) + (yu + yd), drift))
        p, zz, side, drift = terms[0]
        s, zz_s, side_s, drift_s = terms[1]
        drive = p * (1.0 - p) * (0.4 * p + 0.2 * s - 0.4)
        change = 0.15 * zz + 0.1 * side - 0.7 * p - drift + drive
        out_p.append(p + change)
        out_s.append(0.4 * s + 0.1 * (zz_s + side_s) - drift_s + 0.85 * s * change)
    return out_p, out_s


def finish(
    vel, p_low, s_low, p1, s1, fine, hx_high, hy_high,
    vel_out, p_out, s_out, p_high, s_high, sems,
):
    copies = [
        pltpu.make_async_copy(vel, vel_out, sems.at[0]),
        pltpu.make_async_copy(p_low, p_out.at[0:16], sems.at[1]),
        pltpu.make_async_copy(s_low, s_out.at[0:16], sems.at[2]),
    ]
    for copy in copies:
        copy.start()
    sides = tuple(pltpu.roll(hy_high[i], 112, 1) for i in range(2))
    for part in range(2):

        def step(k, carry):
            results = plane(k + 16, (p1, s1), fine, hx_high, k, carry)
            for dst, (left, right) in zip((p_high, s_high), results):
                dst[k, :, :128] = left
                dst[k, :, 128:] = right
            return next_sides(carry)

        sides = lax.fori_loop(8 * part, 8 * part + 8, step, sides)
        here = slice(8 * part, 8 * part + 8)
        there = slice(16 + 8 * part, 24 + 8 * part)
        for n, (src, dst) in enumerate(((p_high, p_out), (s_high, s_out))):
            copy = pltpu.make_async_copy(
                src.at[here], dst.at[there], sems.at[3 + 2 * part + n]
            )
            copy.start()
            copies.append(copy)
    for copy in copies:
        copy.wait()


def body(slabs, lanes, populations, field_gain, front_depth, phase, solute):
    depth_here, rows_here, cols = populations.shape[1:]
    pops = populations.reshape(19, depth_here * rows_here, cols)
    vmem = pl.BlockSpec(memory_space=pltpu.VMEM)
    anywhere = pl.BlockSpec(memory_space=pltpu.HBM)
    copies = 8 + 4 + 2 + (slabs - 1) + 8
    passed = pl.pallas_call(
        functools.partial(kernel, slabs, lanes),
        out_shape=(
            jax.ShapeDtypeStruct((3, 128, 128), F32),
            jax.ShapeDtypeStruct((16, 32, 256), F32),
            jax.ShapeDtypeStruct((16, 32, 256), F32),
            jax.ShapeDtypeStruct(phase.shape, F32),
            jax.ShapeDtypeStruct(solute.shape, F32),
            jax.ShapeDtypeStruct((3, 6, 32, 256), F32),
            jax.ShapeDtypeStruct((2, 2, 16, 256), F32),
            jax.ShapeDtypeStruct((2, 32, 128), F32),
        ),
        in_specs=[anywhere] * 8,
        out_specs=(vmem,) * 8,
        scratch_shapes=[
            pltpu.VMEM(pops.shape, F32),
            pltpu.VMEM((1, depth_here), F32),
            pltpu.SMEM(front_depth.shape, jnp.int32),
            pltpu.VMEM(phase.shape, F32),
            pltpu.VMEM(solute.shape, F32),
            pltpu.VMEM((3, 8, cols), F32),
            pltpu.VMEM((128, 512), F32),
            pltpu.VMEM((32, 8), F32),
            pltpu.VMEM((14, 128, 128), F32),
            pltpu.VMEM((2, 128, 128), F32),
            pltpu.VMEM((2, 128, 128), F32),
            pltpu.VMEM((2, 4, 8, 128), F32),
            pltpu.VMEM((4, 8, 128), F32),
            pltpu.VMEM((2, 128, 128), F32),
            pltpu.VMEM((2, 128, 128), F32),
            pltpu.VMEM((3, 2, 16, 8, 128), F32),
            pltpu.VMEM((3, 2, 16, 8, 128), F32),
            pltpu.VMEM((slabs, 9, 8, 128), F32),
            pltpu.VMEM((slabs - 1, 9, 8, 128), F32),
            pltpu.VMEM((2, 2, 2, 32, 256), F32),
            pltpu.VMEM((2, 2, 2, 32, 256), F32),
            pltpu.VMEM((3, 2, 32, 128), F32),
            pltpu.VMEM((3, 2, 32, 128), F32),
            pltpu.SemaphoreType.DMA((copies,)),
            pltpu.SemaphoreType.DMA((copies,)),
            pltpu.SemaphoreType.DMA((8,)),
        ],
        compiler_params=pltpu.CompilerParams(
            collective_id=0, has_side_effects=True, vmem_limit_bytes=24 * 2**20
        ),
    )(
        *(pltpu.with_memory_space_constraint(x, pltpu.HBM) for x in (pops,
        field_gain.reshape(1, depth_here),
        front_depth,
        phase,
        solute,
        jnp.asarray(force_table(lanes, cols)),
        jnp.asarray(col_table()),
        jnp.asarray(row_table())))
    )
    velocity, phase_next, solute_next = pl.pallas_call(
        finish,
        out_shape=(
            jax.ShapeDtypeStruct((3, 128, 128), F32),
            jax.ShapeDtypeStruct(phase.shape, F32),
            jax.ShapeDtypeStruct(solute.shape, F32),
        ),
        in_specs=[vmem] * 8,
        out_specs=(anywhere,) * 3,
        scratch_shapes=[
            pltpu.VMEM((16, 32, 256), F32),
            pltpu.VMEM((16, 32, 256), F32),
            pltpu.SemaphoreType.DMA((7,)),
        ],
        compiler_params=pltpu.CompilerParams(vmem_limit_bytes=16 * 2**20),
    )(*passed)
    return velocity.reshape(3, depth_here, rows_here, cols), phase_next, solute_next


def solution(mesh):
    return jax.shard_map(
        functools.partial(body, mesh.shape["gz"], mesh.shape["xy"]),
        mesh=mesh,
        in_specs=(
            P(None, "gz", "xy", None),
            P("gz"),
            P("xy", None),
            P(None, "xy", "gz"),
            P(None, "xy", "gz"),
        ),
        out_specs=(P(None, "gz", "xy", None), P(None, "xy", "gz"), P(None, "xy", "gz")),
        check_vma=False,
    )
```

```python
import functools
import math

import jax
import jax.numpy as jnp
import numpy as np
from jax import lax
from jax.experimental import pallas as pl
from jax.experimental.pallas import tpu as pltpu
from jax.sharding import PartitionSpec as P

MESH = pl.DeviceIdType.MESH
F32 = jnp.float32

PAIRS = (
    (1, 2, (1, 0, 0), 1.0 / 18.0),
    (3, 4, (0, 1, 0), 1.0 / 18.0),
    (5, 6, (0, 0, 1), 1.0 / 18.0),
    (7, 8, (1, 1, 0), 1.0 / 36.0),
    (9, 10, (1, -1, 0), 1.0 / 36.0),
    (11, 12, (1, 0, 1), 1.0 / 36.0),
    (13, 14, (1, 0, -1), 1.0 / 36.0),
    (15, 16, (0, 1, 1), 1.0 / 36.0),
    (17, 18, (0, 1, -1), 1.0 / 36.0),
)


def weights_of(fine):
    numer = 2 * fine + 9
    return numer // 16, (numer % 16) / 16.0


def col_table():
    table = np.zeros((128, 512), np.float32)
    for par in range(2):
        for fine in range(256):
            tile, inner = fine // 32, fine % 32
            low, frac = weights_of(inner)
            for off, weight in ((low, 1.0 - frac), (low + 1, frac)):
                if off == 0:
                    rim, j = 1, 0
                elif off == 5:
                    rim, j = 1, 3
                else:
                    rim, j = 0, off - 1
                table[par * 64 + rim * 32 + tile * 4 + j, par * 256 + fine] += weight
    return table


def row_table():
    table = np.zeros((32, 8), np.float32)
    for fine in range(32):
        low, frac = weights_of(fine)
        for off, weight in ((low, 1.0 - frac), (low + 1, frac)):
            place = 4 if off == 0 else off if off == 5 else off - 1
            table[fine, place] += 0.2 * weight
    return table


def force_table(lanes, width_y):
    width_x = 4 * lanes
    x = (np.arange(width_x) + 0.5) * (2.0 * math.pi / width_x)
    y = (np.arange(width_y) + 0.5) * (2.0 * math.pi / width_y)
    ax = np.tile(x.reshape(lanes, 4), (1, 2))[:, :, None]
    ay = y[None, None, :]
    full = (lanes, 8, width_y)
    return np.stack(
        [
            np.broadcast_to(np.cos(ax - 0.7), full),
            np.broadcast_to(np.sin(ay + 0.7), full),
            np.cos(ax + ay),
        ],
        axis=1,
    ).astype(np.float32)


def kernel(
    slabs, lanes,
    pop_hbm, gain_hbm, depth_hbm, phase_hbm, solute_hbm, ftab_hbm, ctab_hbm, rtab_hbm,
    vel, p_low, s_low, p1, s1, fine, hx_high, hy_high,
    pop, gain, depth, phase, solute, ftab, ctab, rtab,
    sums, xs, xr, zr, dr, vs, vr, v8, v8r, pk, wr, ex, hx, ey, hy,
    send, recv, local,
):
    gz, xy = lax.axis_index("gz"), lax.axis_index("xy")
    loads = []
    for src, dst in (
        (gain_hbm, gain), (ftab_hbm.at[xy], ftab), (pop_hbm, pop), (depth_hbm, depth),
        (phase_hbm, phase), (solute_hbm, solute), (ctab_hbm, ctab), (rtab_hbm, rtab),
    ):
        load = pltpu.make_async_copy(src, dst, local.at[len(loads)])
        load.start()
        loads.append(load)

    def at(dz, dx):
        return (lax.rem(gz + dz + slabs, slabs), lax.rem(xy + dx + lanes, lanes))

    peers = [(1, 0), (-1, 0), (0, 1), (0, -1), (1, 1), (1, -1), (-1, 1), (-1, -1)]
    peers += [(d, 0) for d in range(2, slabs - 1)]
    barrier = pltpu.get_barrier_semaphore()
    for peer in peers:
        pl.semaphore_signal(barrier, inc=1, device_id=at(*peer), device_id_type=MESH)

    count = [0]

    def remote(src, dst, where):
        i = count[0]
        count[0] += 1
        copy = pltpu.make_async_remote_copy(
            src_ref=src, dst_ref=dst, send_sem=send.at[i], recv_sem=recv.at[i],
            device_id=at(*where), device_id_type=MESH,
        )
        copy.start()
        return copy

    for load in loads[:3]:
        load.wait()
    rows32 = lax.broadcasted_iota(jnp.int32, (128, 32), 0) // 4
    cols32 = lax.broadcasted_iota(jnp.int32, (128, 32), 1)
    gain_col = jnp.sum(jnp.where(rows32 == cols32, gain[...], 0.0), axis=1, keepdims=True)
    shape = ftab[...]
    force = [
        jnp.broadcast_to(shape[c][None], (16, 8, 128)).reshape(128, 128) * gain_col
        for c in range(3)
    ]
    for c in range(3):
        vel[c] = force[c]

    def collide(i, carry):
        at_rows = pl.ds(pl.multiple_of(i * 8, 8), 8)
        f = [pop[q, at_rows, :] for q in range(19)]
        fc = [vel[c, at_rows, :] for c in range(3)]
        rho = f[0]
        mom = [0.5 * fc[0], 0.5 * fc[1], 0.5 * fc[2]]
        for a, b, e, _ in PAIRS:
            rho = rho + (f[a] + f[b])
            odd = f[a] - f[b]
            for c in range(3):
                if e[c] > 0:
                    mom[c] = mom[c] + odd
                elif e[c] < 0:
                    mom[c] = mom[c] - odd
        inv = 1.0 / rho
        u = [m * inv for m in mom]
        speed = u[0] * u[0] + u[1] * u[1] + u[2] * u[2]
        work = u[0] * fc[0] + u[1] * fc[1] + u[2] * fc[2]
        base = 1.25 * rho * (1.0 - 1.5 * speed) - 1.125 * work
        rho_a = 5.625 * rho
        rho_b = 3.75 * rho
        post = [None] * 19
        post[0] = -0.25 * f[0] + (1.0 / 3.0) * base

        def along(v, e):
            total = None
            for c in range(3):
                if e[c]:
                    term = v[c] if e[c] > 0 else -v[c]
                    total = term if total is None else total + term
            return total

        for a, b, e, w in PAIRS:
            cu, cf = along(u, e), along(fc, e)
            even = w * (base + cu * (rho_a * cu + 3.375 * cf))
            odd = w * (rho_b * cu + 1.125 * cf)
            post[a] = -0.25 * f[a] + (even + odd)
            post[b] = -0.25 * f[b] + (even - odd)

        def up(q):
            return pltpu.roll(post[q], 1, 1)

        def down(q):
            return pltpu.roll(post[q], 127, 1)

        def put(n, middle, plus, minus):
            a, b = up(plus), down(minus)
            sums[n, at_rows, :] = post[middle] + (a + b)
            sums[n + 1, at_rows, :] = a - b

        put(0, 1, 11, 13)
        sums[2, at_rows, :] = post[7]
        sums[3, at_rows, :] = post[9]
        put(4, 2, 14, 12)
        sums[6, at_rows, :] = post[10]
        sums[7, at_rows, :] = post[8]
        put(8, 3, 15, 17)
        put(10, 4, 18, 16)
        put(12, 0, 5, 6)
        return carry

    lax.fori_loop(0, 16, collide, 0, unroll=2)

    row = lax.broadcasted_iota(jnp.int32, (128, 128), 0)
    x_of = lax.rem(row, 4)
    plus_ids, minus_ids = (8, 9, 2, 6), (10, 11, 3, 7)

    def roll0(v, s):
        s = s % v.shape[0]
        return v if s == 0 else pltpu.roll(v, s, 0)

    def merge(values):
        out = values[-1]
        for m in range(len(values) - 1):
            out = jnp.where(x_of == m, values[m], out)
        return out

    xs[0] = merge([roll0(sums[i], m - 3) for m, i in enumerate(plus_ids)])
    xs[1] = merge([roll0(sums[i], m) for m, i in enumerate(minus_ids)])

    pl.semaphore_wait(barrier, len(peers))
    flow_copies = [
        remote(xs.at[0], xr.at[0], (0, 1)),
        remote(xs.at[1], xr.at[1], (0, -1)),
        remote(sums.at[pl.ds(0, 4), pl.ds(120, 8)], zr.at[0], (1, 0)),
        remote(sums.at[pl.ds(4, 4), pl.ds(0, 8)], zr.at[1], (-1, 0)),
        remote(sums.at[2, pl.ds(120, 8)], dr.at[0], (1, 1)),
        remote(sums.at[3, pl.ds(120, 8)], dr.at[1], (1, -1)),
        remote(sums.at[6, pl.ds(0, 8)], dr.at[2], (-1, 1)),
        remote(sums.at[7, pl.ds(0, 8)], dr.at[3], (-1, -1)),
    ]

    for load in loads[3:]:
        load.wait()
    lane = lax.broadcasted_iota(jnp.int32, (32, 128), 1)

    def edges(k, carry):
        first, last = carry
        for n, ref in enumerate((phase, solute)):
            ex[0, 0, n, pl.ds(k, 1), :] = ref[k, 31:32, :]
            ex[0, 1, n, pl.ds(k, 1), :] = ref[k, 0:1, :]
            here = lane == k + 32 * n
            last = jnp.where(here, ref[k, :, 255:256], last)
            first = jnp.where(here, ref[k, :, 0:1], first)
        return first, last

    nothing = jnp.zeros((32, 128), F32)
    first, last = lax.fori_loop(0, 32, edges, (nothing, nothing), unroll=4)
    ey[0, 0] = last
    ey[0, 1] = first

    band_copies = [
        remote(ex.at[0, 0], hx.at[0, 0], (0, 1)),
        remote(ex.at[0, 1], hx.at[0, 1], (0, -1)),
        remote(ey.at[0, 0], hy.at[0, 0], (1, 0)),
        remote(ey.at[0, 1], hy.at[0, 1], (-1, 0)),
    ]
    for copy in flow_copies:
        copy.wait()

    sub = lax.broadcasted_iota(jnp.int32, (8, 128), 0)

    def shift_x(i, sign):
        if sign > 0:
            m = plus_ids.index(i)
            return jnp.where(x_of == 0, roll0(xr[0], -m), roll0(sums[i], 1))
        m = minus_ids.index(i)
        return jnp.where(x_of == 3, roll0(xr[1], 3 - m), roll0(sums[i], -1))

    def shift_z(value, sign, block):
        moved = roll0(value, 4 * sign)
        if sign > 0:
            return jnp.concatenate([jnp.where(sub < 4, block, moved[:8]), moved[8:]], axis=0)
        return jnp.concatenate([moved[:120], jnp.where(sub >= 4, block, moved[120:])], axis=0)

    rho = sums[12]
    my = sums[13]
    a = shift_x(8, 1)
    b = shift_x(10, -1)
    rho = rho + (a + b)
    mx = a - b
    my = my + (shift_x(9, 1) + shift_x(11, -1))
    a = shift_z(sums[0], 1, roll0(zr[0, 0], 4))
    b = shift_z(sums[4], -1, roll0(zr[1, 0], 4))
    rho = rho + (a + b)
    mz = a - b
    my = my + shift_z(sums[1], 1, roll0(zr[0, 1], 4))
    my = my + shift_z(sums[5], -1, roll0(zr[1, 1], 4))
    a = shift_z(shift_x(2, 1), 1, jnp.where(sub == 0, roll0(dr[0], 1), roll0(zr[0, 2], 5)))
    b = shift_z(shift_x(7, -1), -1, jnp.where(sub == 7, roll0(dr[3], 7), roll0(zr[1, 3], 3)))
    rho = rho + (a + b)
    mz = mz + (a - b)
    mx = mx + (a - b)
    a = shift_z(shift_x(3, -1), 1, jnp.where(sub == 3, roll0(dr[1], 7), roll0(zr[0, 3], 3)))
    b = shift_z(shift_x(6, 1), -1, jnp.where(sub == 4, roll0(dr[2], 1), roll0(zr[1, 2], 5)))
    rho = rho + (a + b)
    mz = mz + (a - b)
    mx = mx - (a - b)
    inv = 1.0 / rho
    v = [(m + 0.5 * vel[c]) * inv for c, m in enumerate((mz, mx, my))]
    for c in range(3):
        vel[c] = v[c]
    vs[0] = merge([roll0(v[c], c - 3) for c in range(3)])
    vs[1] = merge([roll0(v[c], c) for c in range(3)])
    rim_copies = [
        remote(vs.at[0], vr.at[0], (0, 1)),
        remote(vs.at[1], vr.at[1], (0, -1)),
    ]
    for copy in rim_copies:
        copy.wait()

    sub128 = lax.rem(row, 8)
    lane128 = lax.broadcasted_iota(jnp.int32, (128, 128), 1)
    lane_in = lax.rem(lane128, 4)
    for c in range(3):
        own = vel[c]
        for par in range(2):
            block = jnp.where(
                sub128 == 4,
                roll0(vr[0], 4 - c - 4 * par),
                jnp.where(sub128 == 5, roll0(vr[1], 5 - c - 4 * par), roll0(own, -4 * par)),
            )
            v8[c, par] = block.reshape(16, 8, 128)
            side = jnp.where(lane_in == 0, pltpu.roll(block, 1, 1), pltpu.roll(block, 127, 1))
            v8r[c, par] = side.reshape(16, 8, 128)

    lane8 = lax.broadcasted_iota(jnp.int32, (8, 128), 1)
    tile_of = lane8 // 4
    group_of = lane8 // 32
    tiles_z = 8 * slabs
    none8 = jnp.zeros((8, 128), F32)

    def gather(tile, carry):
        here_z = depth[0, tile]
        prev_z = jnp.where(here_z == 0, tiles_z - 1, here_z - 1)
        next_z = jnp.where(here_z == tiles_z - 1, 0, here_z + 1)
        masks, places = [], []
        for at_tile in (prev_z, here_z, next_z):
            masks.append(tile_of == jnp.where((at_tile >> 3) == gz, tile, -1))
            places.append((at_tile & 7) * 2)
        picks = [(0, 1, places[0] + 1)]
        picks += [(1, i % 2, places[1] + i // 2) for i in range(4)]
        picks += [(2, 0, places[2])]
        out = []
        for c in range(3):
            for dz, (m, par, half) in enumerate(picks):
                out.append(jnp.where(masks[m], v8[c, par, half], carry[12 * c + 2 * dz]))
                out.append(jnp.where(masks[m], v8r[c, par, half], carry[12 * c + 2 * dz + 1]))
        return tuple(out)

    items = lax.fori_loop(0, 8 * slabs, gather, (none8,) * 36, unroll=4)
    for c in range(3):
        for target in range(slabs):
            for m in range(3):
                out = none8
                for g in range(4):
                    item = items[12 * c + 4 * m + g]
                    s = (32 * (g - target)) % 128
                    moved = item if s == 0 else pltpu.roll(item, s, 1)
                    out = jnp.where(group_of == g, moved, out)
                pk[target, 3 * c + m] = out

    window_copies = [
        remote(pk.at[lax.rem(gz + d, slabs)], wr.at[d - 1], (d, 0)) for d in range(1, slabs)
    ]
    windows = pk[gz]
    for d, copy in enumerate(window_copies):
        copy.wait()
        windows = windows + wr[d]
    wide = jnp.dot(
        windows.reshape(72, 128), ctab[...],
        precision=lax.Precision.HIGHEST, preferred_element_type=F32,
    )
    for c in range(3):
        for dz in range(6):
            at_row = (3 * c + dz // 2) * 8
            at_col = (dz % 2) * 256
            fine[c, dz] = jnp.dot(
                rtab[...], wide[at_row:at_row + 8, at_col:at_col + 256],
                precision=lax.Precision.HIGHEST, preferred_element_type=F32,
            )

    def keep_edges(k, results, carry):
        last, first = carry
        for n, (left, right) in enumerate(results):
            ex[1, 0, n, pl.ds(k, 1), :] = jnp.concatenate([left[31:32], right[31:32]], axis=1)
            ex[1, 1, n, pl.ds(k, 1), :] = jnp.concatenate([left[0:1], right[0:1]], axis=1)
            here = lane == k + 32 * n
            last = jnp.where(here, right[:, 127:128], last)
            first = jnp.where(here, left[:, 0:1], first)
        return last, first

    for copy in band_copies:
        copy.wait()
    sides = (hy[0, 0], hy[0, 1])
    halves = []
    for half in range(2):
        ks = slice(16 * half, 16 * half + 16)

        def first_step(k, carry):
            results = plane(k, (phase, solute), fine, hx.at[0], k, carry[:2])
            for dst, (left, right) in zip((p1, s1), results):
                dst[k, :, :128] = left
                dst[k, :, 128:] = right
            return next_sides(carry[:2]) + keep_edges(k, results, carry[2:])

        *sides, last, first = lax.fori_loop(
            16 * half, 16 * half + 16, first_step, (*sides, nothing, nothing), unroll=2
        )
        ey[1 + half, 0] = last
        ey[1 + half, 1] = first
        halves.append([
            remote(ex.at[1, 0, :, ks], hx.at[1, 0, :, ks], (0, 1)),
            remote(ex.at[1, 1, :, ks], hx.at[1, 1, :, ks], (0, -1)),
            remote(ey.at[1 + half, 0], hy.at[1 + half, 0], (1, 0)),
            remote(ey.at[1 + half, 1], hy.at[1 + half, 1], (-1, 0)),
        ])
    for copy in halves[0]:
        copy.wait()

    def second_step(k, carry):
        results = plane(k, (p1, s1), fine, hx.at[1], k, carry)
        for dst, (left, right) in zip((p_low, s_low), results):
            dst[k, :, :128] = left
            dst[k, :, 128:] = right
        return next_sides(carry)

    lax.fori_loop(0, 16, second_step, (hy[1, 0], hy[1, 1]), unroll=2)
    for copy in halves[1]:
        copy.wait()
    hx_high[...] = hx[1, :, :, 16:32]
    hy_high[...] = hy[2]


def next_sides(sides):
    return tuple(pltpu.roll(v, 127, 1) for v in sides)


def plane(k, src, fine, rows, row_at, sides):
    sub = lax.broadcasted_iota(jnp.int32, (32, 128), 0)
    lane = lax.broadcasted_iota(jnp.int32, (32, 128), 1)
    before, after = sides
    low = (2 * k + 9) >> 4
    frac = ((2 * k + 9) & 15).astype(F32) * (1.0 / 16.0)
    above, below = jnp.minimum(k + 1, 31), jnp.maximum(k - 1, 0)
    along_y = []
    for n, ref in enumerate(src):
        left, right = ref[k, :, :128], ref[k, :, 128:]
        left_up, right_up = pltpu.roll(left, 127, 1), pltpu.roll(right, 127, 1)
        left_dn, right_dn = pltpu.roll(left, 1, 1), pltpu.roll(right, 1, 1)
        edge_up, edge_dn = after[:, 32 * n:32 * n + 1], before[:, 32 * n:32 * n + 1]
        along_y.append((
            (jnp.where(lane == 127, right_up, left_up), jnp.where(lane == 0, edge_dn, left_dn)),
            (jnp.where(lane == 127, edge_up, right_up), jnp.where(lane == 0, left_dn, right_dn)),
        ))
    out_p, out_s = [], []
    for half in range(2):
        cols = slice(128 * half, 128 * half + 128)
        flow = []
        for c in range(3):
            lower = fine[c, low, :, cols]
            flow.append(lower + frac * (fine[c, low + 1, :, cols] - lower))
        terms = []
        for n, ref in enumerate(src):
            mid = ref[k, :, cols]
            zu, zd = ref[above, :, cols], ref[below, :, cols]
            row_up = rows[1, n, pl.ds(row_at, 1), :][:, cols]
            row_dn = rows[0, n, pl.ds(row_at, 1), :][:, cols]
            xu = jnp.where(sub == 31, row_up, pltpu.roll(mid, 31, 0))
            xd = jnp.where(sub == 0, row_dn, pltpu.roll(mid, 1, 0))
            yu, yd = along_y[n][half]
            drift = flow[0] * (zu - zd) + flow[1] * (xu - xd) + flow[2] * (yu - yd)
            terms.append((mid, zu + zd, (xu + xd) + (yu + yd), drift))
        p, zz, side, drift = terms[0]
        s, zz_s, side_s, drift_s = terms[1]
        drive = p * (1.0 - p) * (0.4 * p + 0.2 * s - 0.4)
        change = 0.15 * zz + 0.1 * side - 0.7 * p - drift + drive
        out_p.append(p + change)
        out_s.append(0.4 * s + 0.1 * (zz_s + side_s) - drift_s + 0.85 * s * change)
    return out_p, out_s


def finish(
    vel, p_low, s_low, p1, s1, fine, hx_high, hy_high,
    vel_out, p_out, s_out, p_high, s_high, sems,
):
    copies = [
        pltpu.make_async_copy(vel, vel_out, sems.at[0]),
        pltpu.make_async_copy(p_low, p_out.at[0:16], sems.at[1]),
        pltpu.make_async_copy(s_low, s_out.at[0:16], sems.at[2]),
    ]
    for copy in copies:
        copy.start()
    sides = tuple(pltpu.roll(hy_high[i], 112, 1) for i in range(2))
    for part in range(2):

        def step(k, carry):
            results = plane(k + 16, (p1, s1), fine, hx_high, k, carry)
            for dst, (left, right) in zip((p_high, s_high), results):
                dst[k, :, :128] = left
                dst[k, :, 128:] = right
            return next_sides(carry)

        sides = lax.fori_loop(8 * part, 8 * part + 8, step, sides, unroll=2)
        here = slice(8 * part, 8 * part + 8)
        there = slice(16 + 8 * part, 24 + 8 * part)
        for n, (src, dst) in enumerate(((p_high, p_out), (s_high, s_out))):
            copy = pltpu.make_async_copy(
                src.at[here], dst.at[there], sems.at[3 + 2 * part + n]
            )
            copy.start()
            copies.append(copy)
    for copy in copies:
        copy.wait()


def body(slabs, lanes, populations, field_gain, front_depth, phase, solute):
    depth_here, rows_here, cols = populations.shape[1:]
    pops = populations.reshape(19, depth_here * rows_here, cols)
    vmem = pl.BlockSpec(memory_space=pltpu.VMEM)
    anywhere = pl.BlockSpec(memory_space=pltpu.HBM)
    copies = 8 + 4 + 2 + (slabs - 1) + 8
    passed = pl.pallas_call(
        functools.partial(kernel, slabs, lanes),
        out_shape=(
            jax.ShapeDtypeStruct((3, 128, 128), F32),
            jax.ShapeDtypeStruct((16, 32, 256), F32),
            jax.ShapeDtypeStruct((16, 32, 256), F32),
            jax.ShapeDtypeStruct(phase.shape, F32),
            jax.ShapeDtypeStruct(solute.shape, F32),
            jax.ShapeDtypeStruct((3, 6, 32, 256), F32),
            jax.ShapeDtypeStruct((2, 2, 16, 256), F32),
            jax.ShapeDtypeStruct((2, 32, 128), F32),
        ),
        in_specs=[anywhere] * 8,
        out_specs=(vmem,) * 8,
        scratch_shapes=[
            pltpu.VMEM(pops.shape, F32),
            pltpu.VMEM((1, depth_here), F32),
            pltpu.SMEM(front_depth.shape, jnp.int32),
            pltpu.VMEM(phase.shape, F32),
            pltpu.VMEM(solute.shape, F32),
            pltpu.VMEM((3, 8, cols), F32),
            pltpu.VMEM((128, 512), F32),
            pltpu.VMEM((32, 8), F32),
            pltpu.VMEM((14, 128, 128), F32),
            pltpu.VMEM((2, 128, 128), F32),
            pltpu.VMEM((2, 128, 128), F32),
            pltpu.VMEM((2, 4, 8, 128), F32),
            pltpu.VMEM((4, 8, 128), F32),
            pltpu.VMEM((2, 128, 128), F32),
            pltpu.VMEM((2, 128, 128), F32),
            pltpu.VMEM((3, 2, 16, 8, 128), F32),
            pltpu.VMEM((3, 2, 16, 8, 128), F32),
            pltpu.VMEM((slabs, 9, 8, 128), F32),
            pltpu.VMEM((slabs - 1, 9, 8, 128), F32),
            pltpu.VMEM((2, 2, 2, 32, 256), F32),
            pltpu.VMEM((2, 2, 2, 32, 256), F32),
            pltpu.VMEM((3, 2, 32, 128), F32),
            pltpu.VMEM((3, 2, 32, 128), F32),
            pltpu.SemaphoreType.DMA((copies,)),
            pltpu.SemaphoreType.DMA((copies,)),
            pltpu.SemaphoreType.DMA((8,)),
        ],
        compiler_params=pltpu.CompilerParams(
            collective_id=0, has_side_effects=True, vmem_limit_bytes=24 * 2**20
        ),
    )(
        *(pltpu.with_memory_space_constraint(x, pltpu.HBM) for x in (pops,
        field_gain.reshape(1, depth_here),
        front_depth,
        phase,
        solute,
        jnp.asarray(force_table(lanes, cols)),
        jnp.asarray(col_table()),
        jnp.asarray(row_table())))
    )
    velocity, phase_next, solute_next = pl.pallas_call(
        finish,
        out_shape=(
            jax.ShapeDtypeStruct((3, 128, 128), F32),
            jax.ShapeDtypeStruct(phase.shape, F32),
            jax.ShapeDtypeStruct(solute.shape, F32),
        ),
        in_specs=[vmem] * 8,
        out_specs=(anywhere,) * 3,
        scratch_shapes=[
            pltpu.VMEM((16, 32, 256), F32),
            pltpu.VMEM((16, 32, 256), F32),
            pltpu.SemaphoreType.DMA((7,)),
        ],
        compiler_params=pltpu.CompilerParams(vmem_limit_bytes=16 * 2**20),
    )(*passed)
    return velocity.reshape(3, depth_here, rows_here, cols), phase_next, solute_next


def solution(mesh):
    return jax.shard_map(
        functools.partial(body, mesh.shape["gz"], mesh.shape["xy"]),
        mesh=mesh,
        in_specs=(
            P(None, "gz", "xy", None),
            P("gz"),
            P("xy", None),
            P(None, "xy", "gz"),
            P(None, "xy", "gz"),
        ),
        out_specs=(P(None, "gz", "xy", None), P(None, "xy", "gz"), P(None, "xy", "gz")),
        check_vma=False,
    )
```
